32 devices in a mesh: groups: 2 (over y), space: 4 (over z), dp: 2 (over x), chan: 2 (over core).
Axes of the slice: x: 2, y: 2, z: 4, core: 2. Of those that a mesh axis runs over, the one named last changes fastest.
Arguments:
- features: bfloat16 [4, 1024, 256], P(('groups', 'dp'), 'space'), parts along dimension 0, may hold values from -40 to 40
- neighbours: int32 [27, 2048], P(None, ('groups', 'space')), parts along dimension 1, may hold values from 0 to 384, as said below
- send_rows: int32 [32, 32], P(('groups', 'space')), parts along dimension 0, may hold values from 0 to 256, as said below
- noise_level: int32 [4], P(('groups', 'dp')), parts along dimension 0, may hold values from 0 to 999
- conv_weight: bfloat16 [27, 256, 256], P(None, None, 'chan'), may hold values from -0.078125 to 0.078125
- out_weight: bfloat16 [256, 256], P(None, 'chan'), may hold values from -0.375 to 0.375
- scale_table: float32 [1000, 256], P(None, 'chan'), may hold values from 0.1 to 1.9
- shift_table: float32 [1000, 256], P(None, 'chan'), may hold values from -3 to 3
- cotangent: bfloat16 [4, 1024, 256], P(('groups', 'dp'), 'space', 'chan'), parts along dimension 0, may hold values from -6 to 6
Outputs:
- mixed: bfloat16 [4, 1024, 256], P(('groups', 'dp'), 'space', 'chan'), parts along dimension 0
- grad_input: bfloat16 [4, 1024, 256], P(('groups', 'dp'), 'space', 'chan'), parts along dimension 0
- grad_weight: bfloat16 [54, 256, 256], P('groups', 'dp', 'chan'), parts along dimension 0
The draws below stay inside these ranges and needn't reach their ends.
There are 2 independent parts, one for each index of `groups`. The reference program is written for one: setup_inputs(seed, part) draws one part's arguments, and reference() takes and returns one part's arrays. A program takes and returns all parts, laid end to end along the dimension named above; an argument that names none is the same for every part. Nothing has to cross between parts.
Inputs may be any that keep to these rules, and one draw needn't show every extreme that they name: neighbours[13, b] is the block's own row. Values below 256 are own rows; a value 256 + s * 32 + j is halo slot j from owner s and is always a filled slot; 384 means no neighbour. `send_rows`: row s * 4 + d holds in its first entries the rows that owner s sends to owner d, then 256 for unused slots; an owner sends nothing to itself; owners next to each other along space send 32 rows to each other, and in every draw some owner receives 32 rows from every other owner.
All inputs are finite; a program needn't handle non-finite values.
Results may differ from the reference program's by a relative error of at most 0.007.
Values may be sent and summed in bfloat16 or wider, within the bound.
A program may use at most 64 MiB of HBM per device.

```python
import math
import jax
import jax.numpy as jnp
from jax import lax

C = 256
LEVELS = 1000
GS = 8
OFFSETS = 27
S_DEV = 256
HALO_DEV = 128
HCAP = 32
SITES = 1024
BATCH = 2
N_SPACE = 4


def halo_counts(key):
    key = jax.random.fold_in(key, 101)
    first_key, second_key = jax.random.split(key)
    base_counts = jax.random.randint(first_key, (N_SPACE, N_SPACE), 0, HCAP + 1)
    source = jnp.arange(N_SPACE)[:, None]
    target = jnp.arange(N_SPACE)[None, :]
    full_target = jax.random.randint(second_key, (), 0, N_SPACE)
    adjacent = jnp.abs(source - target) == 1
    counts = jnp.where(adjacent | (target == full_target), HCAP, base_counts)
    return jnp.where(source == target, 0, counts).astype(jnp.int32)


def draw_send_rows(key, part):
    counts = halo_counts(key)
    key = jax.random.fold_in(key, 7)
    picked = jax.random.randint(key, (N_SPACE, N_SPACE, HCAP), 0, S_DEV)
    position = jnp.arange(HCAP)[None, None, :]
    filled = position < counts[:, :, None]
    return jnp.where(filled, picked, S_DEV).reshape(N_SPACE * N_SPACE, HCAP).astype(jnp.int32)


def draw_neighbours(key, part):
    counts = halo_counts(key)
    key = jax.random.fold_in(key, 23)
    kind_key, own_key, source_key, slot_key = jax.random.split(key, 4)
    site = jnp.arange(SITES)
    owner = site // S_DEV
    inner = site % S_DEV
    kind = jax.random.randint(kind_key, (OFFSETS, SITES), 0, 20)
    own_pick = jax.random.randint(own_key, (OFFSETS, SITES), 0, S_DEV)
    source = jax.random.randint(source_key, (OFFSETS, SITES), 0, N_SPACE)
    slot = jax.random.randint(slot_key, (OFFSETS, SITES), 0, HCAP)
    live = slot < counts[source, owner[None, :]]
    missing = S_DEV + HALO_DEV
    halo_pick = jnp.where(live, S_DEV + source * HCAP + slot, missing)
    value = jnp.where(kind < 11, own_pick, jnp.where(kind < 17, halo_pick, missing))
    value = value.at[13].set(inner)
    return value.astype(jnp.int32)


def draw_features(key, part):
    key = jax.random.fold_in(key, 11)
    value_key, row_key, column_key = jax.random.split(key, 3)
    position = jnp.arange(SITES, dtype=jnp.float32) / SITES
    rising = 0.5 * jnp.exp(jnp.log(3.0) * position)[None, :, None]
    row_scale = rising * jnp.exp(jax.random.uniform(row_key, (BATCH, SITES, 1), jnp.float32, -0.7, 0.7))
    column_scale = jnp.exp(jax.random.uniform(column_key, (1, 1, C), jnp.float32, -1.1, 1.1))
    values = jnp.clip(jax.random.normal(value_key, (BATCH, SITES, C), jnp.float32), -4.0, 4.0)
    return (values * row_scale * column_scale).astype(jnp.bfloat16)


def block_scale(rng, extent, cuts, smallest, high):
    gain = 1.0
    for dim, parts in cuts:
        draws = jax.random.uniform(jax.random.fold_in(jax.random.fold_in(rng, 6), dim), (parts,), jnp.float32, smallest / len(cuts), high / len(cuts))
        gain = gain * jnp.repeat(jnp.exp(draws), extent[dim] // parts).reshape((-1,) + (1,) * (len(extent) - 1 - dim))
    return gain


def scatter_about(key, dims, spread, bound, cuts=(), kind=jnp.bfloat16):
    values = spread * jax.random.normal(key, dims, jnp.float32)
    if cuts:
        values = values * block_scale(key, dims, cuts, -0.22, 0.18)
    return jnp.clip(values, -bound, bound).astype(kind)


def setup_inputs(seed: int = 0, part: int = 0) -> dict:
    seeds = jax.random.split(jax.random.key(seed), 10)
    part_keys = jax.random.split(jax.random.fold_in(seeds[9], part), 10)
    features = draw_features(jax.random.fold_in(jax.random.fold_in(seeds[9], part), 71), part)
    neighbours = draw_neighbours(jax.random.fold_in(jax.random.fold_in(seeds[9], part), 71), part)
    send_rows = draw_send_rows(jax.random.fold_in(jax.random.fold_in(seeds[9], part), 71), part)
    noise_level = jax.random.randint(part_keys[3], (BATCH,), 0, LEVELS).astype(jnp.int32)
    conv_weight = scatter_about(seeds[4], (OFFSETS, C, C), (OFFSETS * C) ** -0.5, 0.078125, ((2, 2),))
    out_weight = scatter_about(seeds[5], (C, C), C ** -0.5, 0.375, ((1, 2),))
    scale_table = jnp.clip(1.0 + 0.18 * jax.random.normal(seeds[6], (LEVELS, C), jnp.float32), 0.1, 1.9)
    shift_table = scatter_about(seeds[7], (LEVELS, C), 0.5, 3.0, ((1, 2),), jnp.float32)
    cotangent = scatter_about(part_keys[8], (BATCH, SITES, C), 1.0, 6.0, ((0, 2), (1, 4), (2, 2)))
    return {"features": features, "neighbours": neighbours, "send_rows": send_rows, "noise_level": noise_level, "conv_weight": conv_weight, "out_weight": out_weight, "scale_table": scale_table, "shift_table": shift_table, "cotangent": cotangent}


EPSILON = 1e-05

def local_index(neighbours, send_rows):
    owners = jnp.arange(N_SPACE, dtype=jnp.int32)
    own_index = owners[:, None] * S_DEV + jnp.arange(S_DEV, dtype=jnp.int32)[None, :]
    sent = send_rows.reshape(N_SPACE, N_SPACE, HCAP)
    source = owners[:, None, None] * S_DEV + sent
    halo_index = jnp.where(sent < S_DEV, source, SITES).astype(jnp.int32)
    halo_index = jnp.transpose(halo_index, (1, 0, 2)).reshape(N_SPACE, HALO_DEV)
    blank = jnp.full((N_SPACE, 1), SITES, jnp.int32)
    local_map = jnp.concatenate([own_index, halo_index, blank], axis=1)
    picks = neighbours.reshape(OFFSETS, N_SPACE, S_DEV)
    global_index = local_map[owners[None, :, None], picks]
    return global_index.reshape(OFFSETS, SITES).astype(jnp.int32)

def reference(features, neighbours, send_rows, noise_level, conv_weight, out_weight, scale_table, shift_table, cotangent):
    global_index = local_index(neighbours, send_rows)
    padded = jnp.concatenate([features, jnp.zeros((BATCH, 1, C), features.dtype)], axis=1)

    def conv_step(total, inputs):
        index_row, weight = inputs
        rows = padded[:, index_row].reshape(BATCH * SITES, C)
        return (total + jnp.dot(rows, weight, preferred_element_type=jnp.float32), None)
    conv_out, _ = lax.scan(conv_step, jnp.zeros((BATCH * SITES, C), jnp.float32), (global_index, conv_weight))
    grouped = conv_out.reshape(BATCH, SITES, C // GS, GS)
    entries = SITES * GS
    group_mean = lax.optimization_barrier(jnp.sum(grouped, axis=(1, 3))) / entries
    group_sq = lax.optimization_barrier(jnp.sum(grouped * grouped, axis=(1, 3))) / entries
    group_var = group_sq - group_mean * group_mean
    inv_std = lax.rsqrt(group_var + EPSILON)
    centred = (grouped - group_mean[:, None, :, None]) * inv_std[:, None, :, None]
    gain_row = scale_table[noise_level]
    shift_row = shift_table[noise_level]
    centred_flat = centred.reshape(BATCH, SITES, C)
    normed = centred_flat * gain_row[:, None, :] + shift_row[:, None, :]
    hidden = jax.nn.silu(normed).astype(jnp.bfloat16)
    mixed_part = jnp.dot(hidden.reshape(-1, C), out_weight, preferred_element_type=jnp.float32).reshape(BATCH, SITES, C)
    mixed = (features.astype(jnp.float32) + mixed_part).astype(jnp.bfloat16)
    grad_hidden = jnp.dot(cotangent.reshape(-1, C), out_weight.T, preferred_element_type=jnp.float32).reshape(BATCH, SITES, C)
    sigmoid_val = jax.nn.sigmoid(normed)
    grad_normed = grad_hidden * sigmoid_val * (1.0 + normed * (1.0 - sigmoid_val))
    grad_centred = (grad_normed * gain_row[:, None, :]).reshape(BATCH, SITES, C // GS, GS)
    sum_grad = lax.optimization_barrier(jnp.sum(grad_centred, axis=(1, 3)))
    sum_cross = lax.optimization_barrier(jnp.sum(grad_centred * centred, axis=(1, 3)))
    grad_conv = inv_std[:, None, :, None] * (grad_centred - sum_grad[:, None, :, None] / entries - centred * (sum_cross / entries)[:, None, :, None])
    grad_flat = grad_conv.reshape(BATCH * SITES, C).astype(jnp.bfloat16)

    def back_step(grad_pad, inputs):
        index_row, weight = inputs
        rows = padded[:, index_row].reshape(BATCH * SITES, C)
        weight_grad = jnp.dot(rows.T, grad_flat, preferred_element_type=jnp.float32)
        contrib = jnp.dot(grad_flat, weight.T, preferred_element_type=jnp.float32).reshape(BATCH, SITES, C)
        grad_pad = grad_pad.at[:, index_row].add(contrib)
        return (grad_pad, weight_grad)
    grad_pad, weight_grads = lax.scan(back_step, jnp.zeros((BATCH, SITES + 1, C), jnp.float32), (global_index, conv_weight))
    grad_weight = (weight_grads * (1.0 / math.sqrt(BATCH * SITES))).astype(jnp.bfloat16)
    grad_input = (grad_pad[:, :SITES] + cotangent.astype(jnp.float32)).astype(jnp.bfloat16)
    return (mixed, grad_input, grad_weight)
```

```python
import functools
import math

import jax
import jax.numpy as jnp
from jax import lax
from jax.experimental import pallas as pl
from jax.experimental.pallas import tpu as pltpu
from jax.sharding import PartitionSpec as P

GS = 8


EPSILON = 1e-05


def on_device(
    features,
    neighbours,
    send_rows,
    noise_level,
    conv_weight,
    out_weight,
    scale_table,
    shift_table,
    cotangent,
):
    own_rows = features[0]
    row_count = own_rows.shape[0]
    channels = own_rows.shape[1]
    half_width = conv_weight.shape[2]
    core_index = lax.axis_index("chan")
    space_count = lax.axis_size("space")
    padded = jnp.concatenate([own_rows, jnp.zeros((1, channels), own_rows.dtype)], axis=0)
    targets = send_rows.reshape(-1)
    outgoing = padded[targets]
    arrived = lax.all_to_all(outgoing, "space", split_axis=0, concat_axis=0, tiled=True)
    halo_rows = arrived.shape[0]
    row_table = jnp.concatenate(
        [own_rows, arrived, jnp.zeros((1, channels), own_rows.dtype)], axis=0
    )
    gathered = row_table[neighbours]
    conv_out = jnp.einsum("ksc,kcd->sd", gathered, conv_weight, preferred_element_type=jnp.float32)
    group_count = half_width // GS
    entries = row_count * space_count * GS
    grouped = conv_out.reshape(row_count, group_count, GS)
    sum_first, sum_second = lax.psum(
        (jnp.sum(grouped, axis=(0, 2)), jnp.sum(grouped * grouped, axis=(0, 2))), "space"
    )
    group_mean = sum_first / entries
    group_var = sum_second / entries - group_mean * group_mean
    inv_std = lax.rsqrt(group_var + EPSILON)
    centred = (grouped - group_mean[None, :, None]) * inv_std[None, :, None]
    noise_row = noise_level[0]
    gain_row = lax.dynamic_index_in_dim(scale_table, noise_row, 0, keepdims=False)
    shift_row = lax.dynamic_index_in_dim(shift_table, noise_row, 0, keepdims=False)
    normed = centred.reshape(row_count, half_width) * gain_row[None, :] + shift_row[None, :]
    hidden = jax.nn.silu(normed).astype(jnp.bfloat16)
    hidden_full = lax.all_gather(hidden, "chan", axis=1, tiled=True)
    mixed_part = jnp.dot(hidden_full, out_weight, preferred_element_type=jnp.float32)
    residual_in = lax.dynamic_slice_in_dim(own_rows, core_index * half_width, half_width, 1).astype(
        jnp.float32
    )
    mixed = (residual_in + mixed_part).astype(jnp.bfloat16)[None]
    cot_rows = cotangent[0]
    cot_full, weight_full = (
        lax.all_gather(cot_rows, "chan", axis=1, tiled=True),
        lax.all_gather(out_weight, "chan", axis=1, tiled=True),
    )
    weight_rows = lax.dynamic_slice_in_dim(weight_full, core_index * half_width, half_width, 0)
    grad_hidden = lax.dot_general(
        cot_full, weight_rows, (((1,), (1,)), ((), ())), preferred_element_type=jnp.float32
    )
    sigmoid_val = jax.nn.sigmoid(normed)
    grad_normed = grad_hidden * sigmoid_val * (1.0 + normed * (1.0 - sigmoid_val))
    grad_centred = (grad_normed * gain_row[None, :]).reshape(row_count, group_count, GS)
    sum_grad, sum_cross = lax.psum(
        (jnp.sum(grad_centred, axis=(0, 2)), jnp.sum(grad_centred * centred, axis=(0, 2))), "space"
    )
    grad_conv = inv_std[None, :, None] * (
        grad_centred
        - sum_grad[None, :, None] / entries
        - centred * (sum_cross / entries)[None, :, None]
    )
    grad_conv = grad_conv.reshape(row_count, half_width).astype(jnp.bfloat16)
    partial_grad = jnp.einsum(
        "ksc,sd->kcd", gathered, grad_conv, preferred_element_type=jnp.float32
    )
    grad_scale = 1.0 / math.sqrt(lax.axis_size("dp") * row_count * space_count)
    total_grad = lax.psum(partial_grad, ("space", "dp"))
    share_rows = channels // lax.axis_size("dp")
    total_grad = lax.dynamic_slice_in_dim(
        total_grad, lax.axis_index("dp") * share_rows, share_rows, 1
    )
    grad_weight = (total_grad * grad_scale).astype(jnp.bfloat16)
    grad_rows = jnp.einsum(
        "sd,kcd->ksc", grad_conv, conv_weight, preferred_element_type=jnp.float32
    )
    grad_table = (
        jnp.zeros((row_count + halo_rows + 1, channels), jnp.float32).at[neighbours].add(grad_rows)
    )
    returned = lax.all_to_all(
        grad_table[row_count : row_count + halo_rows].astype(jnp.bfloat16),
        "space",
        split_axis=0,
        concat_axis=0,
        tiled=True,
    ).astype(jnp.float32)
    collected = jnp.zeros((row_count + 1, channels), jnp.float32).at[targets].add(returned)
    own_grad = lax.psum_scatter(
        (grad_table[:row_count] + collected[:row_count]).astype(jnp.bfloat16),
        "chan",
        scatter_dimension=1,
        tiled=True,
    ).astype(jnp.float32)
    grad_input = (own_grad + cot_rows.astype(jnp.float32)).astype(jnp.bfloat16)[None]
    return (mixed, grad_input, grad_weight)


BF = jnp.bfloat16
F32 = jnp.float32
MESH = pl.DeviceIdType.MESH
RESIDENT_SHARES = 8


def nn(a, b):
    return lax.dot_general(a, b, (((1,), (0,)), ((), ())), preferred_element_type=F32)


def nt(a, b):
    return lax.dot_general(a, b, (((1,), (1,)), ((), ())), preferred_element_type=F32)


def tn(a, b):
    return lax.dot_general(a, b, (((0,), (0,)), ((), ())), preferred_element_type=F32)


def one_hot(index_row, first, count):
    rows = lax.broadcasted_iota(jnp.int32, (count, index_row.shape[1]), 0) + first
    return jnp.where(rows == index_row, 1.0, 0.0).astype(BF)


def unit_kernel(
    N,
    Q,
    feat_ref,
    nb_ref,
    sr_ref,
    noise_ref,
    w_ref,
    ow_ref,
    scale_ref,
    shift_ref,
    cot_ref,
    mixed_ref,
    gin_ref,
    gw_ref,
    feat_t,
    tab,
    tab_all,
    nb_all,
    r_own,
    r_all,
    out_rows,
    halo_in,
    gath,
    wt,
    gath_all,
    cot_sib,
    ow_sib,
    st_own,
    st_in,
    hid_own,
    hid_sib,
    gc_own,
    gc_all,
    acc,
    hg_own,
    hg_in,
    og,
    og_send,
    og_sib,
    halo_s,
    halo_r,
    nb_s,
    nb_r,
    r_s,
    r_r,
    feat_s,
    feat_r,
    sib_s,
    sib_r,
    st_s,
    st_r,
    gc_s,
    gc_r,
    hg_s,
    hg_r,
):
    S, C = feat_ref.shape
    K = nb_ref.shape[0]
    D = cot_ref.shape[1]
    CAP = sr_ref.shape[1]
    H = N * CAP
    CQ = C // Q
    G = D // GS
    entries = S * N * GS
    s = lax.axis_index("space")
    p = lax.axis_index("dp")
    c = lax.axis_index("chan")
    sibling = {"chan": 1 - c}
    zpeers = [lax.rem(s + i, N) for i in range(1, N)]
    gpeers = []
    for i in range(N):
        for j in range(Q):
            if i or j:
                gpeers.append((lax.rem(s + i, N), lax.rem(p + j, Q)))
    pending = []

    def copy(src, dst, send, recv, where):
        return pltpu.make_async_remote_copy(
            src_ref=src, dst_ref=dst, send_sem=send, recv_sem=recv, device_id=where, device_id_type=MESH
        )

    def push(*args):
        started = copy(*args)
        started.start()
        pending.append(started)

    def rows(i, n):
        return pl.ds(pl.multiple_of(i * n, n), n)

    barrier = pltpu.get_barrier_semaphore()
    pl.semaphore_signal(barrier, inc=1, device_id=sibling, device_id_type=MESH)
    for d, q in gpeers:
        pl.semaphore_signal(barrier, inc=1, device_id={"space": d, "dp": q}, device_id_type=MESH)

    lane_h = lax.broadcasted_iota(jnp.int32, (1, H), 1)
    spread = (
        lax.broadcasted_iota(jnp.int32, (CAP, H), 1) % CAP
        == lax.broadcasted_iota(jnp.int32, (CAP, H), 0)
    ).astype(BF)
    tiled = nn(sr_ref[...].astype(F32).astype(BF), spread)
    keep = lax.broadcasted_iota(jnp.int32, (N, H), 1) // CAP == lax.broadcasted_iota(
        jnp.int32, (N, H), 0
    )
    r_row = jnp.sum(jnp.where(keep, tiled, 0.0), axis=0, keepdims=True).astype(jnp.int32)
    r_own[...] = jnp.broadcast_to(r_row, r_own.shape)
    oh_send = one_hot(r_row, 0, S)
    out_rows[...] = tn(oh_send, feat_ref[...]).astype(BF)
    pl.semaphore_wait(barrier, len(gpeers) + 1)

    for d in zpeers:
        push(
            out_rows.at[rows(d, CAP)], halo_in.at[rows(s, CAP)], halo_s.at[d], halo_r.at[s], {"space": d}
        )
    push(cot_ref, cot_sib, sib_s.at[0], sib_r.at[0], sibling)
    push(ow_ref.at[rows(1 - c, D)], ow_sib, sib_s.at[1], sib_r.at[1], sibling)
    feat_t[...] = feat_ref[...].T
    for d in zpeers:
        push(nb_ref, nb_all.at[s], nb_s.at[d], nb_r.at[s], {"space": d})
        push(r_own, r_all.at[s], r_s.at[d], r_r.at[s], {"space": d})
    for d, q in gpeers:
        push(
            feat_t.at[rows(q, CQ)],
            tab_all.at[s, rows(p, CQ), pl.ds(0, S)],
            feat_s.at[d * Q + q],
            feat_r.at[s * Q + p],
            {"space": d, "dp": q},
        )
    halo_in[rows(s, CAP), :] = jnp.zeros((CAP, C), BF)
    hg_in[rows(s, CAP), :] = jnp.zeros((CAP, C), BF)
    nb_all[s] = nb_ref[...]
    r_all[s] = r_own[...]
    tab_all[s, rows(p, CQ), pl.ds(0, S)] = feat_t[rows(p, CQ), :]
    tab[:, pl.ds(0, S)] = feat_t[...]

    def own_rows_step(k, carry):
        gath[rows(k, C), :] = nn(feat_t[...], one_hot(nb_ref[pl.ds(k, 1), :], 0, S)).astype(BF)
        wt[:, rows(k, C)] = w_ref[k].T
        return carry

    lax.fori_loop(0, K, own_rows_step, 0, unroll=3)

    for d in zpeers:
        copy(
            out_rows.at[rows(d, CAP)], halo_in.at[rows(d, CAP)], halo_s.at[d], halo_r.at[d], {"space": d}
        ).wait_recv()
    halo_t = halo_in[...].T

    def conv_step(k, total):
        part = gath[rows(k, C), :] + nn(halo_t, one_hot(nb_ref[pl.ds(k, 1), :], S, H)).astype(BF)
        gath[rows(k, C), :] = part
        return total + nn(wt[:, rows(k, C)], part)

    conv = lax.fori_loop(0, K, conv_step, jnp.zeros((D, S), F32), unroll=3)

    def fold(v):
        v = jnp.sum(v.reshape(G, GS, S), axis=1)
        total = v[:, :128]
        for i in range(1, S // 128):
            total = total + v[:, i * 128 : (i + 1) * 128]
        return total

    member = (
        lax.broadcasted_iota(jnp.int32, (D, G), 0) // GS == lax.broadcasted_iota(jnp.int32, (D, G), 1)
    ).astype(F32)

    def widen(v):
        v = lax.dot_general(
            member, v, (((1,), (0,)), ((), ())), precision=lax.Precision.HIGHEST, preferred_element_type=F32
        )
        return jnp.concatenate([v] * (S // 128), axis=1)

    def send_sums(turn, first, second):
        st_own[turn, 0] = fold(first)
        st_own[turn, 1] = fold(second)
        for d in zpeers:
            push(
                st_own.at[turn],
                st_in.at[turn, s],
                st_s.at[turn * N + d],
                st_r.at[turn * N + s],
                {"space": d},
            )
        st_in[turn, s] = st_own[turn]

    def take_sums(turn):
        for d in zpeers:
            copy(
                st_own.at[turn],
                st_in.at[turn, d],
                st_s.at[turn * N + d],
                st_r.at[turn * N + d],
                {"space": d},
            ).wait_recv()
        total = st_in[turn, 0]
        for i in range(1, N):
            total = total + st_in[turn, i]
        total = jnp.sum(total, axis=2, keepdims=True)
        return jnp.broadcast_to(total[0], (G, 128)), jnp.broadcast_to(total[1], (G, 128))

    send_sums(0, conv, conv * conv)

    def column(ref):
        row = ref[pl.ds(noise_ref[0], 1), :]
        col = jnp.broadcast_to(row, (128, D)).T
        return jnp.concatenate([col] * (S // 128), axis=1)

    gain = column(scale_ref)
    shift = column(shift_ref)
    copy(cot_ref, cot_sib, sib_s.at[0], sib_r.at[0], sibling).wait_recv()
    copy(ow_ref.at[rows(1 - c, D)], ow_sib, sib_s.at[1], sib_r.at[1], sibling).wait_recv()
    grad_hidden = nt(ow_ref[rows(c, D), :], cot_ref[...]) + nt(ow_sib[...], cot_sib[...])

    sum_first, sum_second = take_sums(0)
    mean = sum_first / entries
    var = sum_second / entries - mean * mean
    inv_std = widen(lax.rsqrt(var + EPSILON))
    centred = (conv - widen(mean)) * inv_std
    normed = centred * gain + shift
    sig = 1.0 / (1.0 + jnp.exp(-normed))
    hid_own[...] = (normed * sig).astype(BF)
    push(hid_own, hid_sib, sib_s.at[2], sib_r.at[2], sibling)
    grad_centred = grad_hidden * sig * (1.0 + normed * (1.0 - sig)) * gain
    send_sums(1, grad_centred, grad_centred * centred)

    copy(hid_own, hid_sib, sib_s.at[2], sib_r.at[2], sibling).wait_recv()
    mixed_ref[...] = (
        feat_ref[:, rows(c, D)].astype(F32)
        + tn(hid_own[...], ow_ref[rows(c, D), :])
        + tn(hid_sib[...], ow_ref[rows(1 - c, D), :])
    ).astype(BF)

    sum_grad, sum_cross = take_sums(1)
    grad_conv = inv_std * (
        grad_centred - widen(sum_grad / entries) - centred * widen(sum_cross / entries)
    )
    gc_own[...] = grad_conv.astype(BF)
    for d, q in gpeers:
        push(
            gc_own,
            gc_all.at[p, :, rows(s, S)],
            gc_s.at[d * Q + q],
            gc_r.at[s * Q + p],
            {"space": d, "dp": q},
        )
    gc_all[p, :, rows(s, S)] = gc_own[...]

    acc[...] = jnp.zeros_like(acc)

    def table_step(k, carry):
        hot = one_hot(nb_ref[pl.ds(k, 1), :], 0, S + H)
        acc[...] += nn(w_ref[k], nt(gc_own[...], hot).astype(BF))
        return carry

    lax.fori_loop(0, K, table_step, 0, unroll=3)
    hg_own[...] = acc[:, S:].T.astype(BF)
    for d in zpeers:
        push(hg_own.at[rows(d, CAP)], hg_in.at[rows(s, CAP)], hg_s.at[d], hg_r.at[s], {"space": d})

    for d in zpeers:
        copy(nb_ref, nb_all.at[d], nb_s.at[d], nb_r.at[d], {"space": d}).wait_recv()
        copy(r_own, r_all.at[d], r_s.at[d], r_r.at[d], {"space": d}).wait_recv()
    for d, q in gpeers:
        copy(
            feat_t.at[rows(q, CQ)],
            tab_all.at[d, rows(q, CQ), pl.ds(0, S)],
            feat_s.at[d * Q + q],
            feat_r.at[d * Q + q],
            {"space": d, "dp": q},
        ).wait_recv()
    for d in range(N):
        total = jnp.zeros((C, H), F32)
        for o in range(N):
            line = r_all[o, 0:1, :]
            move = (o - d) * CAP % H
            if move:
                line = jnp.concatenate([line[:, H - move :], line[:, : H - move]], axis=1)
            line = jnp.where(lane_h // CAP == o, line, S)
            total = total + nn(tab_all[o, :, pl.ds(0, S)], one_hot(line, 0, S))
        tab_all[d, :, pl.ds(S, H)] = total.astype(BF)
    for d in range(N):

        def gather_step(k, carry, d=d):
            part = nn(tab_all[d], one_hot(nb_all[d, pl.ds(k, 1), :], 0, S + H)).astype(BF)
            for q in range(Q):
                gath_all[q, rows(k, CQ), pl.ds(d * S, S)] = part[q * CQ : (q + 1) * CQ]
            return carry

        lax.fori_loop(0, K, gather_step, 0, unroll=3)

    for d in zpeers:
        copy(
            hg_own.at[rows(d, CAP)], hg_in.at[rows(d, CAP)], hg_s.at[d], hg_r.at[d], {"space": d}
        ).wait_recv()
    og[...] = acc[:, :S].T + nn(one_hot(r_own[0:1, :], 0, S), hg_in[...])
    og_send[...] = og[:, rows(1 - c, D)].astype(BF)
    push(og_send, og_sib, sib_s.at[3], sib_r.at[3], sibling)

    for d, q in gpeers:
        copy(
            gc_own,
            gc_all.at[q, :, rows(d, S)],
            gc_s.at[d * Q + q],
            gc_r.at[d * Q + q],
            {"space": d, "dp": q},
        ).wait_recv()
    scale = 1.0 / math.sqrt(Q * S * N)
    batch = 3 if K % 3 == 0 else 1

    def weight_step(k, carry):
        here = rows(k, batch * CQ)
        total = nt(gath_all[0, here, :], gc_all[0])
        for q in range(1, Q):
            total = total + nt(gath_all[q, here, :], gc_all[q])
        gw_ref[here, :] = (total * scale).astype(BF)
        return carry

    lax.fori_loop(0, K // batch, weight_step, 0)

    copy(og_send, og_sib, sib_s.at[3], sib_r.at[3], sibling).wait_recv()
    gin_ref[...] = (
        og[:, rows(c, D)].astype(BF).astype(F32)
        + og_sib[...].astype(F32)
        + cot_ref[...].astype(F32)
    ).astype(BF)
    for started in pending:
        started.wait_send()


def fused_on_device(
    features,
    neighbours,
    send_rows,
    noise_level,
    conv_weight,
    out_weight,
    scale_table,
    shift_table,
    cotangent,
):
    N = lax.axis_size("space")
    Q = lax.axis_size("dp")
    S, C = features.shape[1:]
    K, _, D = conv_weight.shape
    CAP = send_rows.shape[1]
    H = N * CAP
    CQ = C // Q
    G = D // GS
    vmem = pl.BlockSpec(memory_space=pltpu.VMEM)
    smem = pl.BlockSpec(memory_space=pltpu.SMEM)
    dma = pltpu.SemaphoreType.DMA
    mixed, grad_input, grad_weight = pl.pallas_call(
        functools.partial(unit_kernel, N, Q),
        out_shape=(
            jax.ShapeDtypeStruct((S, D), BF),
            jax.ShapeDtypeStruct((S, D), BF),
            jax.ShapeDtypeStruct((K * CQ, D), BF),
        ),
        in_specs=[vmem, vmem, vmem, smem, vmem, vmem, vmem, vmem, vmem],
        out_specs=(vmem, vmem, vmem),
        scratch_shapes=[
            pltpu.VMEM((C, S), BF),
            pltpu.VMEM((C, S + H), BF),
            pltpu.VMEM((N, C, S + H), BF),
            pltpu.VMEM((N, K, S), jnp.int32),
            pltpu.VMEM((8, H), jnp.int32),
            pltpu.VMEM((N, 8, H), jnp.int32),
            pltpu.VMEM((H, C), BF),
            pltpu.VMEM((H, C), BF),
            pltpu.VMEM((K * C, S), BF),
            pltpu.VMEM((D, K * C), BF),
            pltpu.VMEM((Q, K * CQ, N * S), BF),
            pltpu.VMEM((S, D), BF),
            pltpu.VMEM((D, D), BF),
            pltpu.VMEM((2, 2, G, 128), F32),
            pltpu.VMEM((2, N, 2, G, 128), F32),
            pltpu.VMEM((D, S), BF),
            pltpu.VMEM((D, S), BF),
            pltpu.VMEM((D, S), BF),
            pltpu.VMEM((Q, D, N * S), BF),
            pltpu.VMEM((C, S + H), F32),
            pltpu.VMEM((H, C), BF),
            pltpu.VMEM((H, C), BF),
            pltpu.VMEM((S, C), F32),
            pltpu.VMEM((S, D), BF),
            pltpu.VMEM((S, D), BF),
            dma((N,)),
            dma((N,)),
            dma((N,)),
            dma((N,)),
            dma((N,)),
            dma((N,)),
            dma((N * Q,)),
            dma((N * Q,)),
            dma((4,)),
            dma((4,)),
            dma((2 * N,)),
            dma((2 * N,)),
            dma((N * Q,)),
            dma((N * Q,)),
            dma((N,)),
            dma((N,)),
        ],
        compiler_params=pltpu.CompilerParams(
            collective_id=0, has_side_effects=True, vmem_limit_bytes=52 * 1024 * 1024
        ),
    )(
        features[0],
        neighbours,
        send_rows,
        noise_level,
        conv_weight,
        out_weight,
        scale_table,
        shift_table,
        cotangent[0],
    )
    return mixed[None], grad_input[None], grad_weight.reshape(K, CQ, D)


def solution(mesh):
    in_specs = (
        P(("groups", "dp"), "space", None),
        P(None, ("groups", "space")),
        P(("groups", "space"), None),
        P(("groups", "dp")),
        P(None, None, "chan"),
        P(None, "chan"),
        P(None, "chan"),
        P(None, "chan"),
        P(("groups", "dp"), "space", "chan"),
    )
    out_specs = (
        P(("groups", "dp"), "space", "chan"),
        P(("groups", "dp"), "space", "chan"),
        P("groups", "dp", "chan"),
    )
    fits = mesh.shape["space"] * mesh.shape["dp"] <= RESIDENT_SHARES
    per_device = fused_on_device if fits else on_device
    return jax.shard_map(
        per_device, mesh=mesh, in_specs=in_specs, out_specs=out_specs, check_vma=False
    )
```

```python
import functools
import math

import jax
import jax.numpy as jnp
from jax import lax
from jax.experimental import pallas as pl
from jax.experimental.pallas import tpu as pltpu
from jax.sharding import PartitionSpec as P

GS = 8


EPSILON = 1e-05


def on_device(
    features,
    neighbours,
    send_rows,
    noise_level,
    conv_weight,
    out_weight,
    scale_table,
    shift_table,
    cotangent,
):
    own_rows = features[0]
    row_count = own_rows.shape[0]
    channels = own_rows.shape[1]
    half_width = conv_weight.shape[2]
    core_index = lax.axis_index("chan")
    space_count = lax.axis_size("space")
    padded = jnp.concatenate([own_rows, jnp.zeros((1, channels), own_rows.dtype)], axis=0)
    targets = send_rows.reshape(-1)
    outgoing = padded[targets]
    arrived = lax.all_to_all(outgoing, "space", split_axis=0, concat_axis=0, tiled=True)
    halo_rows = arrived.shape[0]
    row_table = jnp.concatenate(
        [own_rows, arrived, jnp.zeros((1, channels), own_rows.dtype)], axis=0
    )
    gathered = row_table[neighbours]
    conv_out = jnp.einsum("ksc,kcd->sd", gathered, conv_weight, preferred_element_type=jnp.float32)
    group_count = half_width // GS
    entries = row_count * space_count * GS
    grouped = conv_out.reshape(row_count, group_count, GS)
    sum_first, sum_second = lax.psum(
        (jnp.sum(grouped, axis=(0, 2)), jnp.sum(grouped * grouped, axis=(0, 2))), "space"
    )
    group_mean = sum_first / entries
    group_var = sum_second / entries - group_mean * group_mean
    inv_std = lax.rsqrt(group_var + EPSILON)
    centred = (grouped - group_mean[None, :, None]) * inv_std[None, :, None]
    noise_row = noise_level[0]
    gain_row = lax.dynamic_index_in_dim(scale_table, noise_row, 0, keepdims=False)
    shift_row = lax.dynamic_index_in_dim(shift_table, noise_row, 0, keepdims=False)
    normed = centred.reshape(row_count, half_width) * gain_row[None, :] + shift_row[None, :]
    hidden = jax.nn.silu(normed).astype(jnp.bfloat16)
    hidden_full = lax.all_gather(hidden, "chan", axis=1, tiled=True)
    mixed_part = jnp.dot(hidden_full, out_weight, preferred_element_type=jnp.float32)
    residual_in = lax.dynamic_slice_in_dim(own_rows, core_index * half_width, half_width, 1).astype(
        jnp.float32
    )
    mixed = (residual_in + mixed_part).astype(jnp.bfloat16)[None]
    cot_rows = cotangent[0]
    cot_full, weight_full = (
        lax.all_gather(cot_rows, "chan", axis=1, tiled=True),
        lax.all_gather(out_weight, "chan", axis=1, tiled=True),
    )
    weight_rows = lax.dynamic_slice_in_dim(weight_full, core_index * half_width, half_width, 0)
    grad_hidden = lax.dot_general(
        cot_full, weight_rows, (((1,), (1,)), ((), ())), preferred_element_type=jnp.float32
    )
    sigmoid_val = jax.nn.sigmoid(normed)
    grad_normed = grad_hidden * sigmoid_val * (1.0 + normed * (1.0 - sigmoid_val))
    grad_centred = (grad_normed * gain_row[None, :]).reshape(row_count, group_count, GS)
    sum_grad, sum_cross = lax.psum(
        (jnp.sum(grad_centred, axis=(0, 2)), jnp.sum(grad_centred * centred, axis=(0, 2))), "space"
    )
    grad_conv = inv_std[None, :, None] * (
        grad_centred
        - sum_grad[None, :, None] / entries
        - centred * (sum_cross / entries)[None, :, None]
    )
    grad_conv = grad_conv.reshape(row_count, half_width).astype(jnp.bfloat16)
    partial_grad = jnp.einsum(
        "ksc,sd->kcd", gathered, grad_conv, preferred_element_type=jnp.float32
    )
    grad_scale = 1.0 / math.sqrt(lax.axis_size("dp") * row_count * space_count)
    total_grad = lax.psum(partial_grad, ("space", "dp"))
    share_rows = channels // lax.axis_size("dp")
    total_grad = lax.dynamic_slice_in_dim(
        total_grad, lax.axis_index("dp") * share_rows, share_rows, 1
    )
    grad_weight = (total_grad * grad_scale).astype(jnp.bfloat16)
    grad_rows = jnp.einsum(
        "sd,kcd->ksc", grad_conv, conv_weight, preferred_element_type=jnp.float32
    )
    grad_table = (
        jnp.zeros((row_count + halo_rows + 1, channels), jnp.float32).at[neighbours].add(grad_rows)
    )
    returned = lax.all_to_all(
        grad_table[row_count : row_count + halo_rows].astype(jnp.bfloat16),
        "space",
        split_axis=0,
        concat_axis=0,
        tiled=True,
    ).astype(jnp.float32)
    collected = jnp.zeros((row_count + 1, channels), jnp.float32).at[targets].add(returned)
    own_grad = lax.psum_scatter(
        (grad_table[:row_count] + collected[:row_count]).astype(jnp.bfloat16),
        "chan",
        scatter_dimension=1,
        tiled=True,
    ).astype(jnp.float32)
    grad_input = (own_grad + cot_rows.astype(jnp.float32)).astype(jnp.bfloat16)[None]
    return (mixed, grad_input, grad_weight)


BF = jnp.bfloat16
F32 = jnp.float32
MESH = pl.DeviceIdType.MESH
RESIDENT_SHARES = 8


def nn(a, b):
    return lax.dot_general(a, b, (((1,), (0,)), ((), ())), preferred_element_type=F32)


def nt(a, b):
    return lax.dot_general(a, b, (((1,), (1,)), ((), ())), preferred_element_type=F32)


def tn(a, b):
    return lax.dot_general(a, b, (((0,), (0,)), ((), ())), preferred_element_type=F32)


def one_hot(index_row, first, count):
    pieces = []
    for begin in range(first, first + count, 256):
        size = min(256, first + count - begin)
        rows = lax.broadcasted_iota(jnp.int32, (size, index_row.shape[1]), 0).astype(F32).astype(BF)
        line = (index_row - begin).astype(F32).astype(BF)
        hit = rows == jnp.broadcast_to(line, rows.shape)
        pieces.append(jnp.where(hit, jnp.ones_like(rows), jnp.zeros_like(rows)))
    return pieces[0] if len(pieces) == 1 else jnp.concatenate(pieces, axis=0)


def unit_kernel(
    N,
    Q,
    feat_hbm,
    nb_hbm,
    sr_hbm,
    noise_ref,
    w_hbm,
    ow_hbm,
    scale_hbm,
    shift_hbm,
    cot_hbm,
    mixed_ref,
    gin_ref,
    gw_ref,
    feat_ref,
    nb_ref,
    sr_ref,
    w_ref,
    ow_ref,
    scale_ref,
    shift_ref,
    cot_ref,
    load_s,
    feat_t,
    tab_all,
    nb_all,
    r_own,
    r_all,
    out_rows,
    halo_in,
    gath,
    wt,
    gath_all,
    cot_sib,
    ow_sib,
    st_own,
    st_in,
    hid_own,
    hid_sib,
    gc_own,
    gc_all,
    acc,
    hg_own,
    hg_in,
    og,
    og_send,
    og_sib,
    halo_s,
    halo_r,
    nb_s,
    nb_r,
    r_s,
    r_r,
    feat_s,
    feat_r,
    pass_s,
    pass_r,
    sib_s,
    sib_r,
    st_s,
    st_r,
    gc_s,
    gc_r,
    hg_s,
    hg_r,
):
    S, C = feat_ref.shape
    K = nb_ref.shape[0]
    D = cot_ref.shape[1]
    CAP = sr_ref.shape[1]
    H = N * CAP
    CQ = C // Q
    G = D // GS
    entries = S * N * GS
    s = lax.axis_index("space")
    p = lax.axis_index("dp")
    c = lax.axis_index("chan")
    sibling = {"chan": 1 - c}
    zpeers = [lax.rem(s + i, N) for i in range(1, N)]
    gpeers = []
    for i in range(N):
        for j in range(Q):
            if i or j:
                gpeers.append((lax.rem(s + i, N), lax.rem(p + j, Q)))
    pending = []
    batch = 3 if K % 3 == 0 else 1

    def copy(src, dst, send, recv, where):
        return pltpu.make_async_remote_copy(
            src_ref=src, dst_ref=dst, send_sem=send, recv_sem=recv, device_id=where, device_id_type=MESH
        )

    def push(*args):
        started = copy(*args)
        started.start()
        pending.append(started)

    def rows(i, n):
        return pl.ds(pl.multiple_of(i * n, n), n)

    def half(i, core):
        return pl.ds(pl.multiple_of(i * CQ + core * (CQ // 2), CQ // 2), CQ // 2)

    load = [
        pltpu.make_async_copy(src, dst, load_s.at[i])
        for i, (src, dst) in enumerate(
            [
                (sr_hbm, sr_ref),
                (feat_hbm, feat_ref),
                (ow_hbm, ow_ref),
                (cot_hbm, cot_ref),
                (nb_hbm, nb_ref),
                (w_hbm, w_ref),
                (scale_hbm, scale_ref),
                (shift_hbm, shift_ref),
            ]
        )
    ]
    barrier = pltpu.get_barrier_semaphore()
    pl.semaphore_signal(barrier, inc=1, device_id=sibling, device_id_type=MESH)
    for d, q in gpeers:
        pl.semaphore_signal(barrier, inc=1, device_id={"space": d, "dp": q}, device_id_type=MESH)
    for one in load:
        one.start()
    for one in load[:2]:
        one.wait()

    lane_h = lax.broadcasted_iota(jnp.int32, (1, H), 1)
    spread = (
        lax.broadcasted_iota(jnp.int32, (CAP, H), 1) % CAP
        == lax.broadcasted_iota(jnp.int32, (CAP, H), 0)
    ).astype(BF)
    tiled = nn(sr_ref[...].astype(F32).astype(BF), spread)
    keep = lax.broadcasted_iota(jnp.int32, (N, H), 1) // CAP == lax.broadcasted_iota(
        jnp.int32, (N, H), 0
    )
    r_row = jnp.sum(jnp.where(keep, tiled, 0.0), axis=0, keepdims=True).astype(jnp.int32)
    r_own[...] = jnp.broadcast_to(r_row, r_own.shape)
    oh_send = one_hot(r_row, 0, S)
    out_rows[...] = tn(oh_send, feat_ref[...]).astype(BF)
    feat_t[...] = feat_ref[...].T
    for one in load[2:5]:
        one.wait()
    pl.semaphore_wait(barrier, len(gpeers) + 1)

    for d in zpeers:
        push(
            out_rows.at[rows(d, CAP)], halo_in.at[rows(s, CAP)], halo_s.at[d], halo_r.at[s], {"space": d}
        )
    push(cot_ref, cot_sib, sib_s.at[0], sib_r.at[0], sibling)
    push(ow_ref.at[rows(1 - c, D)], ow_sib, sib_s.at[1], sib_r.at[1], sibling)
    for d in zpeers:
        push(nb_ref, nb_all.at[s], nb_s.at[d], nb_r.at[s], {"space": d})
        push(r_own, r_all.at[s], r_s.at[d], r_r.at[s], {"space": d})
    for d, q in gpeers:
        push(
            feat_t.at[half(q, c)],
            tab_all.at[s, half(p, c), pl.ds(0, S)],
            feat_s.at[d * Q + q],
            feat_r.at[s * Q + p],
            {"space": d, "dp": q},
        )
    halo_in[rows(s, CAP), :] = jnp.zeros((CAP, C), BF)
    hg_in[rows(s, CAP), :] = jnp.zeros((CAP, C), BF)
    nb_all[s] = nb_ref[...]
    r_all[s] = r_own[...]
    tab_all[s, rows(p, CQ), pl.ds(0, S)] = feat_t[rows(p, CQ), :]
    load[5].wait()

    def own_rows_step(k, carry):
        gath[rows(k, C), :] = nn(feat_t[...], one_hot(nb_ref[pl.ds(k, 1), :], 0, S)).astype(BF)
        wt[:, rows(k, C)] = w_ref[k].T
        return carry

    lax.fori_loop(0, K, own_rows_step, 0, unroll=3)

    for d in zpeers:
        copy(
            out_rows.at[rows(d, CAP)], halo_in.at[rows(d, CAP)], halo_s.at[d], halo_r.at[d], {"space": d}
        ).wait_recv()
    halo_t = halo_in[...].T

    def conv_step(j, total):
        parts = []
        for i in range(batch):
            hot = one_hot(nb_ref[pl.ds(j * batch + i, 1), :], S, H)
            parts.append(gath[rows(j * batch + i, C), :] + nn(halo_t, hot).astype(BF))
        return total + nn(wt[:, rows(j, batch * C)], jnp.concatenate(parts, axis=0))

    conv = lax.fori_loop(0, K // batch, conv_step, jnp.zeros((D, S), F32))

    def fold(v):
        v = jnp.sum(v.reshape(G, GS, S), axis=1)
        total = v[:, :128]
        for i in range(1, S // 128):
            total = total + v[:, i * 128 : (i + 1) * 128]
        return total

    member = (
        lax.broadcasted_iota(jnp.int32, (D, G), 0) // GS == lax.broadcasted_iota(jnp.int32, (D, G), 1)
    ).astype(F32)

    def widen(v):
        v = lax.dot_general(
            member, v, (((1,), (0,)), ((), ())), precision=lax.Precision.HIGHEST, preferred_element_type=F32
        )
        return jnp.concatenate([v] * (S // 128), axis=1)

    def send_sums(turn, first, second):
        st_own[turn, 0] = fold(first)
        st_own[turn, 1] = fold(second)
        for d in zpeers:
            push(
                st_own.at[turn],
                st_in.at[turn, s],
                st_s.at[turn * N + d],
                st_r.at[turn * N + s],
                {"space": d},
            )
        st_in[turn, s] = st_own[turn]

    def take_sums(turn):
        for d in zpeers:
            copy(
                st_own.at[turn],
                st_in.at[turn, d],
                st_s.at[turn * N + d],
                st_r.at[turn * N + d],
                {"space": d},
            ).wait_recv()
        total = st_in[turn, 0]
        for i in range(1, N):
            total = total + st_in[turn, i]
        total = jnp.sum(total, axis=2, keepdims=True)
        return jnp.broadcast_to(total[0], (G, 128)), jnp.broadcast_to(total[1], (G, 128))

    send_sums(0, conv, conv * conv)

    def column(ref):
        row = ref[pl.ds(noise_ref[0], 1), :]
        col = jnp.broadcast_to(row, (128, D)).T
        return jnp.concatenate([col] * (S // 128), axis=1)

    load[6].wait()
    load[7].wait()
    gain = column(scale_ref)
    shift = column(shift_ref)
    copy(cot_ref, cot_sib, sib_s.at[0], sib_r.at[0], sibling).wait_recv()
    copy(ow_ref.at[rows(1 - c, D)], ow_sib, sib_s.at[1], sib_r.at[1], sibling).wait_recv()
    grad_hidden = nt(ow_ref[rows(c, D), :], cot_ref[...]) + nt(ow_sib[...], cot_sib[...])

    passed = []
    for d in zpeers:
        copy(nb_ref, nb_all.at[d], nb_s.at[d], nb_r.at[d], {"space": d}).wait_recv()
        copy(r_own, r_all.at[d], r_s.at[d], r_r.at[d], {"space": d}).wait_recv()
    for d, q in gpeers:
        mine = tab_all.at[d, half(q, c), pl.ds(0, S)]
        other = tab_all.at[d, half(q, 1 - c), pl.ds(0, S)]
        slot = d * Q + q
        copy(
            feat_t.at[half(q, c)], mine, feat_s.at[slot], feat_r.at[slot], {"space": d, "dp": q}
        ).wait_recv()
        push(mine, mine, pass_s.at[slot], pass_r.at[slot], sibling)
        passed.append(copy(other, other, pass_s.at[slot], pass_r.at[slot], sibling))
    for one in passed:
        one.wait_recv()
    for d in range(N):
        total = jnp.zeros((C, H), F32)
        for o in range(N):
            line = r_all[o, 0:1, :]
            move = (o - d) * CAP % H
            if move:
                line = jnp.concatenate([line[:, H - move :], line[:, : H - move]], axis=1)
            line = jnp.where(lane_h // CAP == o, line, S)
            total = total + nn(tab_all[o, :, pl.ds(0, S)], one_hot(line, 0, S))
        tab_all[d, :, pl.ds(S, H)] = total.astype(BF)

    def gather_rows(owners):
        def gather_step(k, carry):
            for d in owners:
                hot = one_hot(nb_all[d, pl.ds(k, 1), :], 0, S + H)
                part = nn(tab_all[d], hot).astype(BF)
                for q in range(Q):
                    gath_all[q, rows(k, CQ), pl.ds(d * S, S)] = part[q * CQ : (q + 1) * CQ]
            return carry

        lax.fori_loop(0, K, gather_step, 0, unroll=3)

    gather_rows(range(N // 2))

    sum_first, sum_second = take_sums(0)
    mean = sum_first / entries
    var = sum_second / entries - mean * mean
    inv_std = widen(lax.rsqrt(var + EPSILON))
    centred = (conv - widen(mean)) * inv_std
    normed = centred * gain + shift
    sig = 1.0 / (1.0 + jnp.exp(-normed))
    hid_own[...] = (normed * sig).astype(BF)
    push(hid_own, hid_sib, sib_s.at[2], sib_r.at[2], sibling)
    grad_centred = grad_hidden * sig * (1.0 + normed * (1.0 - sig)) * gain
    send_sums(1, grad_centred, grad_centred * centred)

    copy(hid_own, hid_sib, sib_s.at[2], sib_r.at[2], sibling).wait_recv()
    mixed_ref[...] = (
        feat_ref[:, rows(c, D)].astype(F32)
        + tn(hid_own[...], ow_ref[rows(c, D), :])
        + tn(hid_sib[...], ow_ref[rows(1 - c, D), :])
    ).astype(BF)

    gather_rows(range(N // 2, N))

    sum_grad, sum_cross = take_sums(1)
    grad_conv = inv_std * (
        grad_centred - widen(sum_grad / entries) - centred * widen(sum_cross / entries)
    )
    gc_own[...] = grad_conv.astype(BF)
    def pass_over_dp(d, src):
        for q in [lax.rem(p + j, Q) for j in range(1, Q)]:
            push(
                src, gc_all.at[p, :, rows(d, S)], gc_s.at[d * Q + q], gc_r.at[d * Q + p], {"dp": q}
            )

    def gc_arrived(d, q):
        copy(
            gc_own,
            gc_all.at[q, :, rows(d, S)],
            gc_s.at[d * Q + q],
            gc_r.at[d * Q + q],
            {"space": d, "dp": q},
        ).wait_recv()

    for d in zpeers:
        push(gc_own, gc_all.at[p, :, rows(s, S)], gc_s.at[d * Q + p], gc_r.at[s * Q + p], {"space": d})
    pass_over_dp(s, gc_own)
    gc_all[p, :, rows(s, S)] = gc_own[...]

    acc[...] = jnp.zeros_like(acc)

    gc_rows = gc_own[...].T

    def table_step(j, carry):
        sums, weights = [], []
        for i in range(batch):
            hot = one_hot(nb_ref[pl.ds(j * batch + i, 1), :], 0, S + H)
            sums.append(nn(hot, gc_rows).astype(BF))
            weights.append(w_ref[j * batch + i])
        acc[...] += nt(jnp.concatenate(sums, axis=1), jnp.concatenate(weights, axis=1))
        return carry

    steps = K // batch
    early = steps * 5 // 9
    lax.fori_loop(0, early, table_step, 0)
    for d in zpeers:
        gc_arrived(d, p)
        pass_over_dp(d, gc_all.at[p, :, rows(d, S)])
    lax.fori_loop(early, steps, table_step, 0)
    hg_own[...] = acc[S:, :].astype(BF)
    for d in zpeers:
        push(hg_own.at[rows(d, CAP)], hg_in.at[rows(s, CAP)], hg_s.at[d], hg_r.at[s], {"space": d})

    for d in zpeers:
        copy(
            hg_own.at[rows(d, CAP)], hg_in.at[rows(d, CAP)], hg_s.at[d], hg_r.at[d], {"space": d}
        ).wait_recv()
    og[...] = acc[:S, :] + nn(one_hot(r_own[0:1, :], 0, S), hg_in[...])
    og_send[...] = og[:, rows(1 - c, D)].astype(BF)
    push(og_send, og_sib, sib_s.at[3], sib_r.at[3], sibling)

    for d, q in [(lax.rem(s + i, N), lax.rem(p + j, Q)) for i in range(N) for j in range(1, Q)]:
        gc_arrived(d, q)
    scale = 1.0 / math.sqrt(Q * S * N)

    def weight_step(k, carry):
        here = rows(k, batch * CQ)
        total = nt(gath_all[0, here, :], gc_all[0])
        for q in range(1, Q):
            total = total + nt(gath_all[q, here, :], gc_all[q])
        gw_ref[here, :] = (total * scale).astype(BF)
        return carry

    lax.fori_loop(0, K // batch, weight_step, 0)

    copy(og_send, og_sib, sib_s.at[3], sib_r.at[3], sibling).wait_recv()
    gin_ref[...] = (
        og[:, rows(c, D)].astype(BF).astype(F32)
        + og_sib[...].astype(F32)
        + cot_ref[...].astype(F32)
    ).astype(BF)
    for started in pending:
        started.wait_send()


def fused_on_device(
    features,
    neighbours,
    send_rows,
    noise_level,
    conv_weight,
    out_weight,
    scale_table,
    shift_table,
    cotangent,
):
    N = lax.axis_size("space")
    Q = lax.axis_size("dp")
    S, C = features.shape[1:]
    K, _, D = conv_weight.shape
    CAP = send_rows.shape[1]
    H = N * CAP
    CQ = C // Q
    G = D // GS
    vmem = pl.BlockSpec(memory_space=pltpu.VMEM)
    hbm = pl.BlockSpec(memory_space=pltpu.HBM)
    smem = pl.BlockSpec(memory_space=pltpu.SMEM)
    dma = pltpu.SemaphoreType.DMA
    mixed, grad_input, grad_weight = pl.pallas_call(
        functools.partial(unit_kernel, N, Q),
        out_shape=(
            jax.ShapeDtypeStruct((S, D), BF),
            jax.ShapeDtypeStruct((S, D), BF),
            jax.ShapeDtypeStruct((K * CQ, D), BF),
        ),
        in_specs=[hbm, hbm, hbm, smem, hbm, hbm, hbm, hbm, hbm],
        out_specs=(vmem, vmem, vmem),
        scratch_shapes=[
            pltpu.VMEM((S, C), BF),
            pltpu.VMEM((K, S), jnp.int32),
            pltpu.VMEM((N, CAP), jnp.int32),
            pltpu.VMEM((K, C, D), BF),
            pltpu.VMEM((C, D), BF),
            pltpu.VMEM(scale_table.shape, F32),
            pltpu.VMEM(scale_table.shape, F32),
            pltpu.VMEM((S, D), BF),
            dma((8,)),
            pltpu.VMEM((C, S), BF),
            pltpu.VMEM((N, C, S + H), BF),
            pltpu.VMEM((N, K, S), jnp.int32),
            pltpu.VMEM((8, H), jnp.int32),
            pltpu.VMEM((N, 8, H), jnp.int32),
            pltpu.VMEM((H, C), BF),
            pltpu.VMEM((H, C), BF),
            pltpu.VMEM((K * C, S), BF),
            pltpu.VMEM((D, K * C), BF),
            pltpu.VMEM((Q, K * CQ, N * S), BF),
            pltpu.VMEM((S, D), BF),
            pltpu.VMEM((D, D), BF),
            pltpu.VMEM((2, 2, G, 128), F32),
            pltpu.VMEM((2, N, 2, G, 128), F32),
            pltpu.VMEM((D, S), BF),
            pltpu.VMEM((D, S), BF),
            pltpu.VMEM((D, S), BF),
            pltpu.VMEM((Q, D, N * S), BF),
            pltpu.VMEM((S + H, C), F32),
            pltpu.VMEM((H, C), BF),
            pltpu.VMEM((H, C), BF),
            pltpu.VMEM((S, C), F32),
            pltpu.VMEM((S, D), BF),
            pltpu.VMEM((S, D), BF),
            dma((N,)),
            dma((N,)),
            dma((N,)),
            dma((N,)),
            dma((N,)),
            dma((N,)),
            dma((N * Q,)),
            dma((N * Q,)),
            dma((N * Q,)),
            dma((N * Q,)),
            dma((4,)),
            dma((4,)),
            dma((2 * N,)),
            dma((2 * N,)),
            dma((N * Q,)),
            dma((N * Q,)),
            dma((N,)),
            dma((N,)),
        ],
        compiler_params=pltpu.CompilerParams(
            collective_id=0, has_side_effects=True, vmem_limit_bytes=60 * 1024 * 1024
        ),
    )(
        features[0],
        neighbours,
        send_rows,
        noise_level,
        conv_weight,
        out_weight,
        scale_table,
        shift_table,
        cotangent[0],
    )
    return mixed[None], grad_input[None], grad_weight.reshape(K, CQ, D)


def solution(mesh):
    in_specs = (
        P(("groups", "dp"), "space", None),
        P(None, ("groups", "space")),
        P(("groups", "space"), None),
        P(("groups", "dp")),
        P(None, None, "chan"),
        P(None, "chan"),
        P(None, "chan"),
        P(None, "chan"),
        P(("groups", "dp"), "space", "chan"),
    )
    out_specs = (
        P(("groups", "dp"), "space", "chan"),
        P(("groups", "dp"), "space", "chan"),
        P("groups", "dp", "chan"),
    )
    fits = mesh.shape["space"] * mesh.shape["dp"] <= RESIDENT_SHARES
    per_device = fused_on_device if fits else on_device
    return jax.shard_map(
        per_device, mesh=mesh, in_specs=in_specs, out_specs=out_specs, check_vma=False
    )
```

```python
import functools
import math

import jax
import jax.numpy as jnp
from jax import lax
from jax.experimental import pallas as pl
from jax.experimental.pallas import tpu as pltpu
from jax.sharding import PartitionSpec as P

GS = 8


EPSILON = 1e-05


def on_device(
    features,
    neighbours,
    send_rows,
    noise_level,
    conv_weight,
    out_weight,
    scale_table,
    shift_table,
    cotangent,
):
    own_rows = features[0]
    row_count = own_rows.shape[0]
    channels = own_rows.shape[1]
    half_width = conv_weight.shape[2]
    core_index = lax.axis_index("chan")
    space_count = lax.axis_size("space")
    padded = jnp.concatenate([own_rows, jnp.zeros((1, channels), own_rows.dtype)], axis=0)
    targets = send_rows.reshape(-1)
    outgoing = padded[targets]
    arrived = lax.all_to_all(outgoing, "space", split_axis=0, concat_axis=0, tiled=True)
    halo_rows = arrived.shape[0]
    row_table = jnp.concatenate(
        [own_rows, arrived, jnp.zeros((1, channels), own_rows.dtype)], axis=0
    )
    gathered = row_table[neighbours]
    conv_out = jnp.einsum("ksc,kcd->sd", gathered, conv_weight, preferred_element_type=jnp.float32)
    group_count = half_width // GS
    entries = row_count * space_count * GS
    grouped = conv_out.reshape(row_count, group_count, GS)
    sum_first, sum_second = lax.psum(
        (jnp.sum(grouped, axis=(0, 2)), jnp.sum(grouped * grouped, axis=(0, 2))), "space"
    )
    group_mean = sum_first / entries
    group_var = sum_second / entries - group_mean * group_mean
    inv_std = lax.rsqrt(group_var + EPSILON)
    centred = (grouped - group_mean[None, :, None]) * inv_std[None, :, None]
    noise_row = noise_level[0]
    gain_row = lax.dynamic_index_in_dim(scale_table, noise_row, 0, keepdims=False)
    shift_row = lax.dynamic_index_in_dim(shift_table, noise_row, 0, keepdims=False)
    normed = centred.reshape(row_count, half_width) * gain_row[None, :] + shift_row[None, :]
    hidden = jax.nn.silu(normed).astype(jnp.bfloat16)
    hidden_full = lax.all_gather(hidden, "chan", axis=1, tiled=True)
    mixed_part = jnp.dot(hidden_full, out_weight, preferred_element_type=jnp.float32)
    residual_in = lax.dynamic_slice_in_dim(own_rows, core_index * half_width, half_width, 1).astype(
        jnp.float32
    )
    mixed = (residual_in + mixed_part).astype(jnp.bfloat16)[None]
    cot_rows = cotangent[0]
    cot_full, weight_full = (
        lax.all_gather(cot_rows, "chan", axis=1, tiled=True),
        lax.all_gather(out_weight, "chan", axis=1, tiled=True),
    )
    weight_rows = lax.dynamic_slice_in_dim(weight_full, core_index * half_width, half_width, 0)
    grad_hidden = lax.dot_general(
        cot_full, weight_rows, (((1,), (1,)), ((), ())), preferred_element_type=jnp.float32
    )
    sigmoid_val = jax.nn.sigmoid(normed)
    grad_normed = grad_hidden * sigmoid_val * (1.0 + normed * (1.0 - sigmoid_val))
    grad_centred = (grad_normed * gain_row[None, :]).reshape(row_count, group_count, GS)
    sum_grad, sum_cross = lax.psum(
        (jnp.sum(grad_centred, axis=(0, 2)), jnp.sum(grad_centred * centred, axis=(0, 2))), "space"
    )
    grad_conv = inv_std[None, :, None] * (
        grad_centred
        - sum_grad[None, :, None] / entries
        - centred * (sum_cross / entries)[None, :, None]
    )
    grad_conv = grad_conv.reshape(row_count, half_width).astype(jnp.bfloat16)
    partial_grad = jnp.einsum(
        "ksc,sd->kcd", gathered, grad_conv, preferred_element_type=jnp.float32
    )
    grad_scale = 1.0 / math.sqrt(lax.axis_size("dp") * row_count * space_count)
    total_grad = lax.psum(partial_grad, ("space", "dp"))
    share_rows = channels // lax.axis_size("dp")
    total_grad = lax.dynamic_slice_in_dim(
        total_grad, lax.axis_index("dp") * share_rows, share_rows, 1
    )
    grad_weight = (total_grad * grad_scale).astype(jnp.bfloat16)
    grad_rows = jnp.einsum(
        "sd,kcd->ksc", grad_conv, conv_weight, preferred_element_type=jnp.float32
    )
    grad_table = (
        jnp.zeros((row_count + halo_rows + 1, channels), jnp.float32).at[neighbours].add(grad_rows)
    )
    returned = lax.all_to_all(
        grad_table[row_count : row_count + halo_rows].astype(jnp.bfloat16),
        "space",
        split_axis=0,
        concat_axis=0,
        tiled=True,
    ).astype(jnp.float32)
    collected = jnp.zeros((row_count + 1, channels), jnp.float32).at[targets].add(returned)
    own_grad = lax.psum_scatter(
        (grad_table[:row_count] + collected[:row_count]).astype(jnp.bfloat16),
        "chan",
        scatter_dimension=1,
        tiled=True,
    ).astype(jnp.float32)
    grad_input = (own_grad + cot_rows.astype(jnp.float32)).astype(jnp.bfloat16)[None]
    return (mixed, grad_input, grad_weight)


BF = jnp.bfloat16
F32 = jnp.float32
MESH = pl.DeviceIdType.MESH
RESIDENT_SHARES = 8


def nn(a, b):
    return lax.dot_general(a, b, (((1,), (0,)), ((), ())), preferred_element_type=F32)


def nt(a, b):
    return lax.dot_general(a, b, (((1,), (1,)), ((), ())), preferred_element_type=F32)


def tn(a, b):
    return lax.dot_general(a, b, (((0,), (0,)), ((), ())), preferred_element_type=F32)


def one_hot(index_row, first, count):
    pieces = []
    for begin in range(first, first + count, 256):
        size = min(256, first + count - begin)
        rows = lax.broadcasted_iota(jnp.int32, (size, index_row.shape[1]), 0).astype(F32).astype(BF)
        line = (index_row - begin).astype(F32).astype(BF)
        hit = rows == jnp.broadcast_to(line, rows.shape)
        pieces.append(jnp.where(hit, jnp.ones_like(rows), jnp.zeros_like(rows)))
    return pieces[0] if len(pieces) == 1 else jnp.concatenate(pieces, axis=0)


def unit_kernel(
    N,
    Q,
    feat_hbm,
    nb_hbm,
    sr_hbm,
    noise_ref,
    w_hbm,
    ow_hbm,
    scale_hbm,
    shift_hbm,
    cot_hbm,
    mixed_ref,
    gin_ref,
    gw_ref,
    feat_ref,
    nb_ref,
    sr_ref,
    w_ref,
    ow_ref,
    scale_ref,
    shift_ref,
    cot_ref,
    load_s,
    feat_t,
    tab_all,
    nb_all,
    r_own,
    r_all,
    out_rows,
    halo_in,
    gath,
    wt,
    gath_all,
    cot_sib,
    ow_sib,
    st_own,
    st_in,
    hid_own,
    hid_sib,
    gc_own,
    gc_all,
    acc,
    hg_own,
    hg_in,
    og,
    og_send,
    og_sib,
    halo_s,
    halo_r,
    nb_s,
    nb_r,
    r_s,
    r_r,
    feat_s,
    feat_r,
    pass_s,
    pass_r,
    sib_s,
    sib_r,
    st_s,
    st_r,
    gc_s,
    gc_r,
    hg_s,
    hg_r,
):
    S, C = feat_ref.shape
    K = nb_ref.shape[0]
    D = cot_ref.shape[1]
    CAP = sr_ref.shape[1]
    H = N * CAP
    CQ = C // Q
    G = D // GS
    entries = S * N * GS
    s = lax.axis_index("space")
    p = lax.axis_index("dp")
    c = lax.axis_index("chan")
    sibling = {"chan": 1 - c}
    zpeers = [lax.rem(s + i, N) for i in range(1, N)]
    gpeers = []
    for i in range(N):
        for j in range(Q):
            if i or j:
                gpeers.append((lax.rem(s + i, N), lax.rem(p + j, Q)))
    pending = []
    batch = 3 if K % 3 == 0 else 1

    def copy(src, dst, send, recv, where):
        return pltpu.make_async_remote_copy(
            src_ref=src, dst_ref=dst, send_sem=send, recv_sem=recv, device_id=where, device_id_type=MESH
        )

    def push(*args):
        started = copy(*args)
        started.start()
        pending.append(started)

    def rows(i, n):
        return pl.ds(pl.multiple_of(i * n, n), n)

    def half(i, core):
        return pl.ds(pl.multiple_of(i * CQ + core * (CQ // 2), CQ // 2), CQ // 2)

    load = [
        pltpu.make_async_copy(src, dst, load_s.at[i])
        for i, (src, dst) in enumerate(
            [
                (sr_hbm, sr_ref),
                (feat_hbm, feat_ref),
                (ow_hbm, ow_ref),
                (cot_hbm, cot_ref),
                (nb_hbm, nb_ref),
                (w_hbm, w_ref),
                (scale_hbm, scale_ref),
                (shift_hbm, shift_ref),
            ]
        )
    ]
    barrier = pltpu.get_barrier_semaphore()
    pl.semaphore_signal(barrier, inc=1, device_id=sibling, device_id_type=MESH)
    for d, q in gpeers:
        pl.semaphore_signal(barrier, inc=1, device_id={"space": d, "dp": q}, device_id_type=MESH)
    for one in load:
        one.start()
    for one in load[:2]:
        one.wait()

    lane_h = lax.broadcasted_iota(jnp.int32, (1, H), 1)
    spread = (
        lax.broadcasted_iota(jnp.int32, (CAP, H), 1) % CAP
        == lax.broadcasted_iota(jnp.int32, (CAP, H), 0)
    ).astype(BF)
    tiled = nn(sr_ref[...].astype(F32).astype(BF), spread)
    keep = lax.broadcasted_iota(jnp.int32, (N, H), 1) // CAP == lax.broadcasted_iota(
        jnp.int32, (N, H), 0
    )
    r_row = jnp.sum(jnp.where(keep, tiled, 0.0), axis=0, keepdims=True).astype(jnp.int32)
    r_own[...] = jnp.broadcast_to(r_row, r_own.shape)
    oh_send = one_hot(r_row, 0, S)
    out_rows[...] = tn(oh_send, feat_ref[...]).astype(BF)
    feat_t[...] = feat_ref[...].T
    for one in load[2:5]:
        one.wait()
    pl.semaphore_wait(barrier, len(gpeers) + 1)

    for d in zpeers:
        push(
            out_rows.at[rows(d, CAP)], halo_in.at[rows(s, CAP)], halo_s.at[d], halo_r.at[s], {"space": d}
        )
    push(cot_ref, cot_sib, sib_s.at[0], sib_r.at[0], sibling)
    push(ow_ref.at[rows(1 - c, D)], ow_sib, sib_s.at[1], sib_r.at[1], sibling)
    for d in zpeers:
        push(nb_ref, nb_all.at[s], nb_s.at[d], nb_r.at[s], {"space": d})
        push(r_own, r_all.at[s], r_s.at[d], r_r.at[s], {"space": d})
    for d, q in gpeers:
        push(
            feat_t.at[half(q, c)],
            tab_all.at[s, half(p, c), pl.ds(0, S)],
            feat_s.at[d * Q + q],
            feat_r.at[s * Q + p],
            {"space": d, "dp": q},
        )
    halo_in[rows(s, CAP), :] = jnp.zeros((CAP, C), BF)
    hg_in[rows(s, CAP), :] = jnp.zeros((CAP, C), BF)
    nb_all[s] = nb_ref[...]
    r_all[s] = r_own[...]
    tab_all[s, rows(p, CQ), pl.ds(0, S)] = feat_t[rows(p, CQ), :]
    load[5].wait()

    def own_rows_step(k, carry):
        gath[rows(k, C), :] = nn(feat_t[...], one_hot(nb_ref[pl.ds(k, 1), :], 0, S)).astype(BF)
        wt[:, rows(k, C)] = w_ref[k].T
        return carry

    lax.fori_loop(0, K, own_rows_step, 0, unroll=3)

    for d in zpeers:
        copy(
            out_rows.at[rows(d, CAP)], halo_in.at[rows(d, CAP)], halo_s.at[d], halo_r.at[d], {"space": d}
        ).wait_recv()
    halo_t = halo_in[...].T

    def conv_step(j, total):
        parts = []
        for i in range(batch):
            hot = one_hot(nb_ref[pl.ds(j * batch + i, 1), :], S, H)
            parts.append(gath[rows(j * batch + i, C), :] + nn(halo_t, hot).astype(BF))
        return total + nn(wt[:, rows(j, batch * C)], jnp.concatenate(parts, axis=0))

    conv = lax.fori_loop(0, K // batch, conv_step, jnp.zeros((D, S), F32))

    def fold(v):
        v = jnp.sum(v.reshape(G, GS, S), axis=1)
        total = v[:, :128]
        for i in range(1, S // 128):
            total = total + v[:, i * 128 : (i + 1) * 128]
        return total

    member = (
        lax.broadcasted_iota(jnp.int32, (D, G), 0) // GS == lax.broadcasted_iota(jnp.int32, (D, G), 1)
    ).astype(F32)

    def widen(v):
        v = lax.dot_general(
            member, v, (((1,), (0,)), ((), ())), precision=lax.Precision.HIGHEST, preferred_element_type=F32
        )
        return jnp.concatenate([v] * (S // 128), axis=1)

    def send_sums(turn, first, second):
        st_own[turn, 0] = fold(first)
        st_own[turn, 1] = fold(second)
        for d in zpeers:
            push(
                st_own.at[turn],
                st_in.at[turn, s],
                st_s.at[turn * N + d],
                st_r.at[turn * N + s],
                {"space": d},
            )
        st_in[turn, s] = st_own[turn]

    def take_sums(turn):
        for d in zpeers:
            copy(
                st_own.at[turn],
                st_in.at[turn, d],
                st_s.at[turn * N + d],
                st_r.at[turn * N + d],
                {"space": d},
            ).wait_recv()
        total = st_in[turn, 0]
        for i in range(1, N):
            total = total + st_in[turn, i]
        total = jnp.sum(total, axis=2, keepdims=True)
        return jnp.broadcast_to(total[0], (G, 128)), jnp.broadcast_to(total[1], (G, 128))

    send_sums(0, conv, conv * conv)

    def column(ref):
        row = ref[pl.ds(noise_ref[0], 1), :]
        col = jnp.broadcast_to(row, (128, D)).T
        return jnp.concatenate([col] * (S // 128), axis=1)

    load[6].wait()
    load[7].wait()
    gain = column(scale_ref)
    shift = column(shift_ref)
    copy(cot_ref, cot_sib, sib_s.at[0], sib_r.at[0], sibling).wait_recv()
    copy(ow_ref.at[rows(1 - c, D)], ow_sib, sib_s.at[1], sib_r.at[1], sibling).wait_recv()
    grad_hidden = nt(ow_ref[rows(c, D), :], cot_ref[...]) + nt(ow_sib[...], cot_sib[...])

    passed = []
    for d in zpeers:
        copy(nb_ref, nb_all.at[d], nb_s.at[d], nb_r.at[d], {"space": d}).wait_recv()
        copy(r_own, r_all.at[d], r_s.at[d], r_r.at[d], {"space": d}).wait_recv()
    for d, q in gpeers:
        mine = tab_all.at[d, half(q, c), pl.ds(0, S)]
        other = tab_all.at[d, half(q, 1 - c), pl.ds(0, S)]
        slot = d * Q + q
        copy(
            feat_t.at[half(q, c)], mine, feat_s.at[slot], feat_r.at[slot], {"space": d, "dp": q}
        ).wait_recv()
        push(mine, mine, pass_s.at[slot], pass_r.at[slot], sibling)
        passed.append(copy(other, other, pass_s.at[slot], pass_r.at[slot], sibling))

    sum_first, sum_second = take_sums(0)
    mean = sum_first / entries
    var = sum_second / entries - mean * mean
    inv_std = widen(lax.rsqrt(var + EPSILON))
    centred = (conv - widen(mean)) * inv_std
    normed = centred * gain + shift
    sig = 1.0 / (1.0 + jnp.exp(-normed))
    hid_own[...] = (normed * sig).astype(BF)
    push(hid_own, hid_sib, sib_s.at[2], sib_r.at[2], sibling)
    grad_centred = grad_hidden * sig * (1.0 + normed * (1.0 - sig)) * gain
    send_sums(1, grad_centred, grad_centred * centred)

    copy(hid_own, hid_sib, sib_s.at[2], sib_r.at[2], sibling).wait_recv()
    mixed_ref[...] = (
        feat_ref[:, rows(c, D)].astype(F32)
        + tn(hid_own[...], ow_ref[rows(c, D), :])
        + tn(hid_sib[...], ow_ref[rows(1 - c, D), :])
    ).astype(BF)

    for one in passed:
        one.wait_recv()
    for d in range(N):
        total = jnp.zeros((C, H), F32)
        for o in range(N):
            line = r_all[o, 0:1, :]
            move = (o - d) * CAP % H
            if move:
                line = jnp.concatenate([line[:, H - move :], line[:, : H - move]], axis=1)
            line = jnp.where(lane_h // CAP == o, line, S)
            total = total + nn(tab_all[o, :, pl.ds(0, S)], one_hot(line, 0, S))
        tab_all[d, :, pl.ds(S, H)] = total.astype(BF)

    def gather_rows(owners):
        def gather_step(k, carry):
            for d in owners:
                hot = one_hot(nb_all[d, pl.ds(k, 1), :], 0, S + H)
                part = nn(tab_all[d], hot).astype(BF)
                for q in range(Q):
                    gath_all[q, rows(k, CQ), pl.ds(d * S, S)] = part[q * CQ : (q + 1) * CQ]
            return carry

        lax.fori_loop(0, K, gather_step, 0, unroll=3)

    gather_rows(range(1))

    sum_grad, sum_cross = take_sums(1)
    grad_conv = inv_std * (
        grad_centred - widen(sum_grad / entries) - centred * widen(sum_cross / entries)
    )
    gc_own[...] = grad_conv.astype(BF)
    def pass_over_dp(d, src):
        for q in [lax.rem(p + j, Q) for j in range(1, Q)]:
            push(
                src, gc_all.at[p, :, rows(d, S)], gc_s.at[d * Q + q], gc_r.at[d * Q + p], {"dp": q}
            )

    def gc_arrived(d, q):
        copy(
            gc_own,
            gc_all.at[q, :, rows(d, S)],
            gc_s.at[d * Q + q],
            gc_r.at[d * Q + q],
            {"space": d, "dp": q},
        ).wait_recv()

    for d in zpeers:
        push(gc_own, gc_all.at[p, :, rows(s, S)], gc_s.at[d * Q + p], gc_r.at[s * Q + p], {"space": d})
    pass_over_dp(s, gc_own)
    gc_all[p, :, rows(s, S)] = gc_own[...]

    acc[...] = jnp.zeros_like(acc)

    gc_rows = gc_own[...].T

    def table_step(j, carry):
        sums, weights = [], []
        for i in range(batch):
            hot = one_hot(nb_ref[pl.ds(j * batch + i, 1), :], 0, S + H)
            sums.append(nn(hot, gc_rows).astype(BF))
            weights.append(w_ref[j * batch + i])
        acc[...] += nt(jnp.concatenate(sums, axis=1), jnp.concatenate(weights, axis=1))
        return carry

    steps = K // batch
    early = steps * 5 // 9
    lax.fori_loop(0, early, table_step, 0)
    gather_rows(range(1, 2))
    for d in zpeers:
        gc_arrived(d, p)
        pass_over_dp(d, gc_all.at[p, :, rows(d, S)])
    lax.fori_loop(early, steps, table_step, 0)
    hg_own[...] = acc[S:, :].astype(BF)
    for d in zpeers:
        push(hg_own.at[rows(d, CAP)], hg_in.at[rows(s, CAP)], hg_s.at[d], hg_r.at[s], {"space": d})
    gather_rows(range(2, N))

    for d in zpeers:
        copy(
            hg_own.at[rows(d, CAP)], hg_in.at[rows(d, CAP)], hg_s.at[d], hg_r.at[d], {"space": d}
        ).wait_recv()
    og[...] = acc[:S, :] + nn(one_hot(r_own[0:1, :], 0, S), hg_in[...])
    og_send[...] = og[:, rows(1 - c, D)].astype(BF)
    push(og_send, og_sib, sib_s.at[3], sib_r.at[3], sibling)

    for d, q in [(lax.rem(s + i, N), lax.rem(p + j, Q)) for i in range(N) for j in range(1, Q)]:
        gc_arrived(d, q)
    scale = 1.0 / math.sqrt(Q * S * N)

    def weight_step(k, carry):
        here = rows(k, batch * CQ)
        total = nt(gath_all[0, here, :], gc_all[0])
        for q in range(1, Q):
            total = total + nt(gath_all[q, here, :], gc_all[q])
        gw_ref[here, :] = (total * scale).astype(BF)
        return carry

    lax.fori_loop(0, K // batch, weight_step, 0)

    copy(og_send, og_sib, sib_s.at[3], sib_r.at[3], sibling).wait_recv()
    gin_ref[...] = (
        og[:, rows(c, D)].astype(BF).astype(F32)
        + og_sib[...].astype(F32)
        + cot_ref[...].astype(F32)
    ).astype(BF)
    for started in pending:
        started.wait_send()


def fused_on_device(
    features,
    neighbours,
    send_rows,
    noise_level,
    conv_weight,
    out_weight,
    scale_table,
    shift_table,
    cotangent,
):
    N = lax.axis_size("space")
    Q = lax.axis_size("dp")
    S, C = features.shape[1:]
    K, _, D = conv_weight.shape
    CAP = send_rows.shape[1]
    H = N * CAP
    CQ = C // Q
    G = D // GS
    vmem = pl.BlockSpec(memory_space=pltpu.VMEM)
    hbm = pl.BlockSpec(memory_space=pltpu.HBM)
    smem = pl.BlockSpec(memory_space=pltpu.SMEM)
    dma = pltpu.SemaphoreType.DMA
    mixed, grad_input, grad_weight = pl.pallas_call(
        functools.partial(unit_kernel, N, Q),
        out_shape=(
            jax.ShapeDtypeStruct((S, D), BF),
            jax.ShapeDtypeStruct((S, D), BF),
            jax.ShapeDtypeStruct((K * CQ, D), BF),
        ),
        in_specs=[hbm, hbm, hbm, smem, hbm, hbm, hbm, hbm, hbm],
        out_specs=(vmem, vmem, vmem),
        scratch_shapes=[
            pltpu.VMEM((S, C), BF),
            pltpu.VMEM((K, S), jnp.int32),
            pltpu.VMEM((N, CAP), jnp.int32),
            pltpu.VMEM((K, C, D), BF),
            pltpu.VMEM((C, D), BF),
            pltpu.VMEM(scale_table.shape, F32),
            pltpu.VMEM(scale_table.shape, F32),
            pltpu.VMEM((S, D), BF),
            dma((8,)),
            pltpu.VMEM((C, S), BF),
            pltpu.VMEM((N, C, S + H), BF),
            pltpu.VMEM((N, K, S), jnp.int32),
            pltpu.VMEM((8, H), jnp.int32),
            pltpu.VMEM((N, 8, H), jnp.int32),
            pltpu.VMEM((H, C), BF),
            pltpu.VMEM((H, C), BF),
            pltpu.VMEM((K * C, S), BF),
            pltpu.VMEM((D, K * C), BF),
            pltpu.VMEM((Q, K * CQ, N * S), BF),
            pltpu.VMEM((S, D), BF),
            pltpu.VMEM((D, D), BF),
            pltpu.VMEM((2, 2, G, 128), F32),
            pltpu.VMEM((2, N, 2, G, 128), F32),
            pltpu.VMEM((D, S), BF),
            pltpu.VMEM((D, S), BF),
            pltpu.VMEM((D, S), BF),
            pltpu.VMEM((Q, D, N * S), BF),
            pltpu.VMEM((S + H, C), F32),
            pltpu.VMEM((H, C), BF),
            pltpu.VMEM((H, C), BF),
            pltpu.VMEM((S, C), F32),
            pltpu.VMEM((S, D), BF),
            pltpu.VMEM((S, D), BF),
            dma((N,)),
            dma((N,)),
            dma((N,)),
            dma((N,)),
            dma((N,)),
            dma((N,)),
            dma((N * Q,)),
            dma((N * Q,)),
            dma((N * Q,)),
            dma((N * Q,)),
            dma((4,)),
            dma((4,)),
            dma((2 * N,)),
            dma((2 * N,)),
            dma((N * Q,)),
            dma((N * Q,)),
            dma((N,)),
            dma((N,)),
        ],
        compiler_params=pltpu.CompilerParams(
            collective_id=0, has_side_effects=True, vmem_limit_bytes=60 * 1024 * 1024
        ),
    )(
        features[0],
        neighbours,
        send_rows,
        noise_level,
        conv_weight,
        out_weight,
        scale_table,
        shift_table,
        cotangent[0],
    )
    return mixed[None], grad_input[None], grad_weight.reshape(K, CQ, D)


def solution(mesh):
    in_specs = (
        P(("groups", "dp"), "space", None),
        P(None, ("groups", "space")),
        P(("groups", "space"), None),
        P(("groups", "dp")),
        P(None, None, "chan"),
        P(None, "chan"),
        P(None, "chan"),
        P(None, "chan"),
        P(("groups", "dp"), "space", "chan"),
    )
    out_specs = (
        P(("groups", "dp"), "space", "chan"),
        P(("groups", "dp"), "space", "chan"),
        P("groups", "dp", "chan"),
    )
    fits = mesh.shape["space"] * mesh.shape["dp"] <= RESIDENT_SHARES
    per_device = fused_on_device if fits else on_device
    return jax.shard_map(
        per_device, mesh=mesh, in_specs=in_specs, out_specs=out_specs, check_vma=False
    )
```

```python
import functools
import math

import jax
import jax.numpy as jnp
from jax import lax
from jax.experimental import pallas as pl
from jax.experimental.pallas import tpu as pltpu
from jax.sharding import PartitionSpec as P

GS = 8


EPSILON = 1e-05


def on_device(
    features,
    neighbours,
    send_rows,
    noise_level,
    conv_weight,
    out_weight,
    scale_table,
    shift_table,
    cotangent,
):
    own_rows = features[0]
    row_count = own_rows.shape[0]
    channels = own_rows.shape[1]
    half_width = conv_weight.shape[2]
    core_index = lax.axis_index("chan")
    space_count = lax.axis_size("space")
    padded = jnp.concatenate([own_rows, jnp.zeros((1, channels), own_rows.dtype)], axis=0)
    targets = send_rows.reshape(-1)
    outgoing = padded[targets]
    arrived = lax.all_to_all(outgoing, "space", split_axis=0, concat_axis=0, tiled=True)
    halo_rows = arrived.shape[0]
    row_table = jnp.concatenate(
        [own_rows, arrived, jnp.zeros((1, channels), own_rows.dtype)], axis=0
    )
    gathered = row_table[neighbours]
    conv_out = jnp.einsum("ksc,kcd->sd", gathered, conv_weight, preferred_element_type=jnp.float32)
    group_count = half_width // GS
    entries = row_count * space_count * GS
    grouped = conv_out.reshape(row_count, group_count, GS)
    sum_first, sum_second = lax.psum(
        (jnp.sum(grouped, axis=(0, 2)), jnp.sum(grouped * grouped, axis=(0, 2))), "space"
    )
    group_mean = sum_first / entries
    group_var = sum_second / entries - group_mean * group_mean
    inv_std = lax.rsqrt(group_var + EPSILON)
    centred = (grouped - group_mean[None, :, None]) * inv_std[None, :, None]
    noise_row = noise_level[0]
    gain_row = lax.dynamic_index_in_dim(scale_table, noise_row, 0, keepdims=False)
    shift_row = lax.dynamic_index_in_dim(shift_table, noise_row, 0, keepdims=False)
    normed = centred.reshape(row_count, half_width) * gain_row[None, :] + shift_row[None, :]
    hidden = jax.nn.silu(normed).astype(jnp.bfloat16)
    hidden_full = lax.all_gather(hidden, "chan", axis=1, tiled=True)
    mixed_part = jnp.dot(hidden_full, out_weight, preferred_element_type=jnp.float32)
    residual_in = lax.dynamic_slice_in_dim(own_rows, core_index * half_width, half_width, 1).astype(
        jnp.float32
    )
    mixed = (residual_in + mixed_part).astype(jnp.bfloat16)[None]
    cot_rows = cotangent[0]
    cot_full, weight_full = (
        lax.all_gather(cot_rows, "chan", axis=1, tiled=True),
        lax.all_gather(out_weight, "chan", axis=1, tiled=True),
    )
    weight_rows = lax.dynamic_slice_in_dim(weight_full, core_index * half_width, half_width, 0)
    grad_hidden = lax.dot_general(
        cot_full, weight_rows, (((1,), (1,)), ((), ())), preferred_element_type=jnp.float32
    )
    sigmoid_val = jax.nn.sigmoid(normed)
    grad_normed = grad_hidden * sigmoid_val * (1.0 + normed * (1.0 - sigmoid_val))
    grad_centred = (grad_normed * gain_row[None, :]).reshape(row_count, group_count, GS)
    sum_grad, sum_cross = lax.psum(
        (jnp.sum(grad_centred, axis=(0, 2)), jnp.sum(grad_centred * centred, axis=(0, 2))), "space"
    )
    grad_conv = inv_std[None, :, None] * (
        grad_centred
        - sum_grad[None, :, None] / entries
        - centred * (sum_cross / entries)[None, :, None]
    )
    grad_conv = grad_conv.reshape(row_count, half_width).astype(jnp.bfloat16)
    partial_grad = jnp.einsum(
        "ksc,sd->kcd", gathered, grad_conv, preferred_element_type=jnp.float32
    )
    grad_scale = 1.0 / math.sqrt(lax.axis_size("dp") * row_count * space_count)
    total_grad = lax.psum(partial_grad, ("space", "dp"))
    share_rows = channels // lax.axis_size("dp")
    total_grad = lax.dynamic_slice_in_dim(
        total_grad, lax.axis_index("dp") * share_rows, share_rows, 1
    )
    grad_weight = (total_grad * grad_scale).astype(jnp.bfloat16)
    grad_rows = jnp.einsum(
        "sd,kcd->ksc", grad_conv, conv_weight, preferred_element_type=jnp.float32
    )
    grad_table = (
        jnp.zeros((row_count + halo_rows + 1, channels), jnp.float32).at[neighbours].add(grad_rows)
    )
    returned = lax.all_to_all(
        grad_table[row_count : row_count + halo_rows].astype(jnp.bfloat16),
        "space",
        split_axis=0,
        concat_axis=0,
        tiled=True,
    ).astype(jnp.float32)
    collected = jnp.zeros((row_count + 1, channels), jnp.float32).at[targets].add(returned)
    own_grad = lax.psum_scatter(
        (grad_table[:row_count] + collected[:row_count]).astype(jnp.bfloat16),
        "chan",
        scatter_dimension=1,
        tiled=True,
    ).astype(jnp.float32)
    grad_input = (own_grad + cot_rows.astype(jnp.float32)).astype(jnp.bfloat16)[None]
    return (mixed, grad_input, grad_weight)


BF = jnp.bfloat16
F32 = jnp.float32
MESH = pl.DeviceIdType.MESH
RESIDENT_SHARES = 8


def nn(a, b):
    return lax.dot_general(a, b, (((1,), (0,)), ((), ())), preferred_element_type=F32)


def nt(a, b):
    return lax.dot_general(a, b, (((1,), (1,)), ((), ())), preferred_element_type=F32)


def tn(a, b):
    return lax.dot_general(a, b, (((0,), (0,)), ((), ())), preferred_element_type=F32)


def one_hot(index_row, first, count):
    pieces = []
    for begin in range(first, first + count, 256):
        size = min(256, first + count - begin)
        rows = lax.broadcasted_iota(jnp.int32, (size, index_row.shape[1]), 0).astype(F32).astype(BF)
        line = (index_row - begin).astype(F32).astype(BF)
        hit = rows == jnp.broadcast_to(line, rows.shape)
        pieces.append(jnp.where(hit, jnp.ones_like(rows), jnp.zeros_like(rows)))
    return pieces[0] if len(pieces) == 1 else jnp.concatenate(pieces, axis=0)


def unit_kernel(
    N,
    Q,
    feat_hbm,
    nb_hbm,
    sr_hbm,
    noise_ref,
    w_hbm,
    ow_hbm,
    scale_hbm,
    shift_hbm,
    cot_hbm,
    mixed_ref,
    gin_ref,
    gw_ref,
    feat_ref,
    nb_ref,
    sr_ref,
    w_ref,
    ow_ref,
    scale_ref,
    shift_ref,
    cot_ref,
    load_s,
    feat_t,
    tab_all,
    nb_all,
    r_own,
    r_all,
    out_rows,
    halo_in,
    gath,
    wt,
    gath_all,
    cot_sib,
    ow_sib,
    st_own,
    st_in,
    hid_own,
    hid_sib,
    gc_own,
    gc_all,
    acc,
    hg_own,
    hg_in,
    og,
    og_send,
    og_sib,
    halo_s,
    halo_r,
    nb_s,
    nb_r,
    r_s,
    r_r,
    feat_s,
    feat_r,
    pass_s,
    pass_r,
    sib_s,
    sib_r,
    st_s,
    st_r,
    gc_s,
    gc_r,
    hg_s,
    hg_r,
):
    S, C = feat_ref.shape
    K = nb_ref.shape[0]
    D = cot_ref.shape[1]
    CAP = sr_ref.shape[1]
    H = N * CAP
    CQ = C // Q
    G = D // GS
    entries = S * N * GS
    s = lax.axis_index("space")
    p = lax.axis_index("dp")
    c = lax.axis_index("chan")
    sibling = {"chan": 1 - c}
    zpeers = [lax.rem(s + i, N) for i in range(1, N)]
    gpeers = []
    for i in range(N):
        for j in range(Q):
            if i or j:
                gpeers.append((lax.rem(s + i, N), lax.rem(p + j, Q)))
    pending = []
    batch = 3 if K % 3 == 0 else 1

    def copy(src, dst, send, recv, where):
        return pltpu.make_async_remote_copy(
            src_ref=src, dst_ref=dst, send_sem=send, recv_sem=recv, device_id=where, device_id_type=MESH
        )

    def push(*args):
        started = copy(*args)
        started.start()
        pending.append(started)

    def rows(i, n):
        return pl.ds(pl.multiple_of(i * n, n), n)

    def half(i, core):
        return pl.ds(pl.multiple_of(i * CQ + core * (CQ // 2), CQ // 2), CQ // 2)

    load = [
        pltpu.make_async_copy(src, dst, load_s.at[i])
        for i, (src, dst) in enumerate(
            [
                (sr_hbm, sr_ref),
                (feat_hbm, feat_ref),
                (ow_hbm, ow_ref),
                (cot_hbm, cot_ref),
                (nb_hbm, nb_ref),
                (w_hbm, w_ref),
                (scale_hbm, scale_ref),
                (shift_hbm, shift_ref),
            ]
        )
    ]
    barrier = pltpu.get_barrier_semaphore()
    pl.semaphore_signal(barrier, inc=1, device_id=sibling, device_id_type=MESH)
    for d, q in gpeers:
        pl.semaphore_signal(barrier, inc=1, device_id={"space": d, "dp": q}, device_id_type=MESH)
    for one in load:
        one.start()
    for one in load[:2]:
        one.wait()

    lane_h = lax.broadcasted_iota(jnp.int32, (1, H), 1)
    spread = (
        lax.broadcasted_iota(jnp.int32, (CAP, H), 1) % CAP
        == lax.broadcasted_iota(jnp.int32, (CAP, H), 0)
    ).astype(BF)
    tiled = nn(sr_ref[...].astype(F32).astype(BF), spread)
    keep = lax.broadcasted_iota(jnp.int32, (N, H), 1) // CAP == lax.broadcasted_iota(
        jnp.int32, (N, H), 0
    )
    r_row = jnp.sum(jnp.where(keep, tiled, 0.0), axis=0, keepdims=True).astype(jnp.int32)
    r_own[...] = jnp.broadcast_to(r_row, r_own.shape)
    oh_send = one_hot(r_row, 0, S)
    out_rows[...] = tn(oh_send, feat_ref[...]).astype(BF)
    feat_t[...] = feat_ref[...].T
    for one in load[2:5]:
        one.wait()
    pl.semaphore_wait(barrier, len(gpeers) + 1)

    for d in zpeers:
        push(
            out_rows.at[rows(d, CAP)], halo_in.at[rows(s, CAP)], halo_s.at[d], halo_r.at[s], {"space": d}
        )
    push(cot_ref, cot_sib, sib_s.at[0], sib_r.at[0], sibling)
    push(ow_ref.at[rows(1 - c, D)], ow_sib, sib_s.at[1], sib_r.at[1], sibling)
    for d in zpeers:
        push(nb_ref, nb_all.at[s], nb_s.at[d], nb_r.at[s], {"space": d})
        push(r_own, r_all.at[s], r_s.at[d], r_r.at[s], {"space": d})
    for d, q in gpeers:
        push(
            feat_t.at[half(q, c)],
            tab_all.at[s, half(p, c), pl.ds(0, S)],
            feat_s.at[d * Q + q],
            feat_r.at[s * Q + p],
            {"space": d, "dp": q},
        )
    halo_in[rows(s, CAP), :] = jnp.zeros((CAP, C), BF)
    hg_in[rows(s, CAP), :] = jnp.zeros((CAP, C), BF)
    nb_all[s] = nb_ref[...]
    r_all[s] = r_own[...]
    tab_all[s, rows(p, CQ), pl.ds(0, S)] = feat_t[rows(p, CQ), :]
    load[5].wait()

    def own_rows_step(k, carry):
        gath[rows(k, C), :] = nn(feat_t[...], one_hot(nb_ref[pl.ds(k, 1), :], 0, S)).astype(BF)
        wt[:, rows(k, C)] = w_ref[k].T
        return carry

    lax.fori_loop(0, K, own_rows_step, 0, unroll=9)

    for d in zpeers:
        copy(
            out_rows.at[rows(d, CAP)], halo_in.at[rows(d, CAP)], halo_s.at[d], halo_r.at[d], {"space": d}
        ).wait_recv()
    halo_t = halo_in[...].T

    def conv_step(j, total):
        parts = []
        for i in range(batch):
            hot = one_hot(nb_ref[pl.ds(j * batch + i, 1), :], S, H)
            parts.append(gath[rows(j * batch + i, C), :] + nn(halo_t, hot).astype(BF))
        return total + nn(wt[:, rows(j, batch * C)], jnp.concatenate(parts, axis=0))

    conv = lax.fori_loop(0, K // batch, conv_step, jnp.zeros((D, S), F32), unroll=3)

    def fold(v):
        v = jnp.sum(v.reshape(G, GS, S), axis=1)
        total = v[:, :128]
        for i in range(1, S // 128):
            total = total + v[:, i * 128 : (i + 1) * 128]
        return total

    member = (
        lax.broadcasted_iota(jnp.int32, (D, G), 0) // GS == lax.broadcasted_iota(jnp.int32, (D, G), 1)
    ).astype(F32)

    def widen(v):
        v = lax.dot_general(
            member, v, (((1,), (0,)), ((), ())), precision=lax.Precision.HIGHEST, preferred_element_type=F32
        )
        return jnp.concatenate([v] * (S // 128), axis=1)

    def send_sums(turn, first, second):
        st_own[turn, 0] = fold(first)
        st_own[turn, 1] = fold(second)
        for d in zpeers:
            push(
                st_own.at[turn],
                st_in.at[turn, s],
                st_s.at[turn * N + d],
                st_r.at[turn * N + s],
                {"space": d},
            )
        st_in[turn, s] = st_own[turn]

    def take_sums(turn):
        for d in zpeers:
            copy(
                st_own.at[turn],
                st_in.at[turn, d],
                st_s.at[turn * N + d],
                st_r.at[turn * N + d],
                {"space": d},
            ).wait_recv()
        total = st_in[turn, 0]
        for i in range(1, N):
            total = total + st_in[turn, i]
        total = jnp.sum(total, axis=2, keepdims=True)
        return jnp.broadcast_to(total[0], (G, 128)), jnp.broadcast_to(total[1], (G, 128))

    send_sums(0, conv, conv * conv)

    def column(ref):
        row = ref[pl.ds(noise_ref[0], 1), :]
        col = jnp.broadcast_to(row, (128, D)).T
        return jnp.concatenate([col] * (S // 128), axis=1)

    load[6].wait()
    load[7].wait()
    gain = column(scale_ref)
    shift = column(shift_ref)
    copy(cot_ref, cot_sib, sib_s.at[0], sib_r.at[0], sibling).wait_recv()
    copy(ow_ref.at[rows(1 - c, D)], ow_sib, sib_s.at[1], sib_r.at[1], sibling).wait_recv()
    grad_hidden = nt(ow_ref[rows(c, D), :], cot_ref[...]) + nt(ow_sib[...], cot_sib[...])

    passed = []
    for d in zpeers:
        copy(nb_ref, nb_all.at[d], nb_s.at[d], nb_r.at[d], {"space": d}).wait_recv()
        copy(r_own, r_all.at[d], r_s.at[d], r_r.at[d], {"space": d}).wait_recv()
    for d, q in gpeers:
        mine = tab_all.at[d, half(q, c), pl.ds(0, S)]
        other = tab_all.at[d, half(q, 1 - c), pl.ds(0, S)]
        slot = d * Q + q
        copy(
            feat_t.at[half(q, c)], mine, feat_s.at[slot], feat_r.at[slot], {"space": d, "dp": q}
        ).wait_recv()
        push(mine, mine, pass_s.at[slot], pass_r.at[slot], sibling)
        passed.append(copy(other, other, pass_s.at[slot], pass_r.at[slot], sibling))

    sum_first, sum_second = take_sums(0)
    mean = sum_first / entries
    var = sum_second / entries - mean * mean
    inv_std = widen(lax.rsqrt(var + EPSILON))
    centred = (conv - widen(mean)) * inv_std
    normed = centred * gain + shift
    sig = 1.0 / (1.0 + jnp.exp(-normed))
    hid_own[...] = (normed * sig).astype(BF)
    push(hid_own, hid_sib, sib_s.at[2], sib_r.at[2], sibling)
    grad_centred = grad_hidden * sig * (1.0 + normed * (1.0 - sig)) * gain
    send_sums(1, grad_centred, grad_centred * centred)

    copy(hid_own, hid_sib, sib_s.at[2], sib_r.at[2], sibling).wait_recv()
    mixed_ref[...] = (
        feat_ref[:, rows(c, D)].astype(F32)
        + tn(hid_own[...], ow_ref[rows(c, D), :])
        + tn(hid_sib[...], ow_ref[rows(1 - c, D), :])
    ).astype(BF)

    for one in passed:
        one.wait_recv()
    for d in range(N):
        total = jnp.zeros((C, H), F32)
        for o in range(N):
            line = r_all[o, 0:1, :]
            move = (o - d) * CAP % H
            if move:
                line = jnp.concatenate([line[:, H - move :], line[:, : H - move]], axis=1)
            line = jnp.where(lane_h // CAP == o, line, S)
            total = total + nn(tab_all[o, :, pl.ds(0, S)], one_hot(line, 0, S))
        tab_all[d, :, pl.ds(S, H)] = total.astype(BF)

    def gather_rows(owners):
        def gather_step(k, carry):
            for d in owners:
                hot = one_hot(nb_all[d, pl.ds(k, 1), :], 0, S + H)
                part = nn(tab_all[d], hot).astype(BF)
                for q in range(Q):
                    gath_all[q, rows(k, CQ), pl.ds(d * S, S)] = part[q * CQ : (q + 1) * CQ]
            return carry

        lax.fori_loop(0, K, gather_step, 0, unroll=9 // len(owners))

    gather_rows(range(1))

    sum_grad, sum_cross = take_sums(1)
    grad_conv = inv_std * (
        grad_centred - widen(sum_grad / entries) - centred * widen(sum_cross / entries)
    )
    gc_own[...] = grad_conv.astype(BF)
    def pass_over_dp(d, src):
        for q in [lax.rem(p + j, Q) for j in range(1, Q)]:
            push(
                src, gc_all.at[p, :, rows(d, S)], gc_s.at[d * Q + q], gc_r.at[d * Q + p], {"dp": q}
            )

    def gc_arrived(d, q):
        copy(
            gc_own,
            gc_all.at[q, :, rows(d, S)],
            gc_s.at[d * Q + q],
            gc_r.at[d * Q + q],
            {"space": d, "dp": q},
        ).wait_recv()

    for d in zpeers:
        push(gc_own, gc_all.at[p, :, rows(s, S)], gc_s.at[d * Q + p], gc_r.at[s * Q + p], {"space": d})
    pass_over_dp(s, gc_own)
    gc_all[p, :, rows(s, S)] = gc_own[...]

    acc[...] = jnp.zeros_like(acc)

    gc_rows = gc_own[...].T

    def table_step(j, carry):
        sums, weights = [], []
        for i in range(batch):
            hot = one_hot(nb_ref[pl.ds(j * batch + i, 1), :], 0, S + H)
            sums.append(nn(hot, gc_rows).astype(BF))
            weights.append(w_ref[j * batch + i])
        acc[...] += nt(jnp.concatenate(sums, axis=1), jnp.concatenate(weights, axis=1))
        return carry

    steps = K // batch
    early = steps * 5 // 9
    lax.fori_loop(0, early, table_step, 0, unroll=2)
    gather_rows(range(1, 2))
    for d in zpeers:
        gc_arrived(d, p)
        pass_over_dp(d, gc_all.at[p, :, rows(d, S)])
    lax.fori_loop(early, steps, table_step, 0, unroll=2)
    hg_own[...] = acc[S:, :].astype(BF)
    for d in zpeers:
        push(hg_own.at[rows(d, CAP)], hg_in.at[rows(s, CAP)], hg_s.at[d], hg_r.at[s], {"space": d})
    gather_rows(range(2, N))

    for d in zpeers:
        copy(
            hg_own.at[rows(d, CAP)], hg_in.at[rows(d, CAP)], hg_s.at[d], hg_r.at[d], {"space": d}
        ).wait_recv()
    og[...] = acc[:S, :] + nn(one_hot(r_own[0:1, :], 0, S), hg_in[...])
    og_send[...] = og[:, rows(1 - c, D)].astype(BF)
    push(og_send, og_sib, sib_s.at[3], sib_r.at[3], sibling)

    for d, q in [(lax.rem(s + i, N), lax.rem(p + j, Q)) for i in range(N) for j in range(1, Q)]:
        gc_arrived(d, q)
    scale = 1.0 / math.sqrt(Q * S * N)

    def weight_step(k, carry):
        here = rows(k, batch * CQ)
        total = nt(gath_all[0, here, :], gc_all[0])
        for q in range(1, Q):
            total = total + nt(gath_all[q, here, :], gc_all[q])
        gw_ref[here, :] = (total * scale).astype(BF)
        return carry

    lax.fori_loop(0, K // batch, weight_step, 0, unroll=3)

    copy(og_send, og_sib, sib_s.at[3], sib_r.at[3], sibling).wait_recv()
    gin_ref[...] = (
        og[:, rows(c, D)].astype(BF).astype(F32)
        + og_sib[...].astype(F32)
        + cot_ref[...].astype(F32)
    ).astype(BF)
    for started in pending:
        started.wait_send()


def fused_on_device(
    features,
    neighbours,
    send_rows,
    noise_level,
    conv_weight,
    out_weight,
    scale_table,
    shift_table,
    cotangent,
):
    N = lax.axis_size("space")
    Q = lax.axis_size("dp")
    S, C = features.shape[1:]
    K, _, D = conv_weight.shape
    CAP = send_rows.shape[1]
    H = N * CAP
    CQ = C // Q
    G = D // GS
    vmem = pl.BlockSpec(memory_space=pltpu.VMEM)
    hbm = pl.BlockSpec(memory_space=pltpu.HBM)
    smem = pl.BlockSpec(memory_space=pltpu.SMEM)
    dma = pltpu.SemaphoreType.DMA
    mixed, grad_input, grad_weight = pl.pallas_call(
        functools.partial(unit_kernel, N, Q),
        out_shape=(
            jax.ShapeDtypeStruct((S, D), BF),
            jax.ShapeDtypeStruct((S, D), BF),
            jax.ShapeDtypeStruct((K * CQ, D), BF),
        ),
        in_specs=[hbm, hbm, hbm, smem, hbm, hbm, hbm, hbm, hbm],
        out_specs=(vmem, vmem, vmem),
        scratch_shapes=[
            pltpu.VMEM((S, C), BF),
            pltpu.VMEM((K, S), jnp.int32),
            pltpu.VMEM((N, CAP), jnp.int32),
            pltpu.VMEM((K, C, D), BF),
            pltpu.VMEM((C, D), BF),
            pltpu.VMEM(scale_table.shape, F32),
            pltpu.VMEM(scale_table.shape, F32),
            pltpu.VMEM((S, D), BF),
            dma((8,)),
            pltpu.VMEM((C, S), BF),
            pltpu.VMEM((N, C, S + H), BF),
            pltpu.VMEM((N, K, S), jnp.int32),
            pltpu.VMEM((8, H), jnp.int32),
            pltpu.VMEM((N, 8, H), jnp.int32),
            pltpu.VMEM((H, C), BF),
            pltpu.VMEM((H, C), BF),
            pltpu.VMEM((K * C, S), BF),
            pltpu.VMEM((D, K * C), BF),
            pltpu.VMEM((Q, K * CQ, N * S), BF),
            pltpu.VMEM((S, D), BF),
            pltpu.VMEM((D, D), BF),
            pltpu.VMEM((2, 2, G, 128), F32),
            pltpu.VMEM((2, N, 2, G, 128), F32),
            pltpu.VMEM((D, S), BF),
            pltpu.VMEM((D, S), BF),
            pltpu.VMEM((D, S), BF),
            pltpu.VMEM((Q, D, N * S), BF),
            pltpu.VMEM((S + H, C), F32),
            pltpu.VMEM((H, C), BF),
            pltpu.VMEM((H, C), BF),
            pltpu.VMEM((S, C), F32),
            pltpu.VMEM((S, D), BF),
            pltpu.VMEM((S, D), BF),
            dma((N,)),
            dma((N,)),
            dma((N,)),
            dma((N,)),
            dma((N,)),
            dma((N,)),
            dma((N * Q,)),
            dma((N * Q,)),
            dma((N * Q,)),
            dma((N * Q,)),
            dma((4,)),
            dma((4,)),
            dma((2 * N,)),
            dma((2 * N,)),
            dma((N * Q,)),
            dma((N * Q,)),
            dma((N,)),
            dma((N,)),
        ],
        compiler_params=pltpu.CompilerParams(
            collective_id=0, has_side_effects=True, vmem_limit_bytes=60 * 1024 * 1024
        ),
    )(
        features[0],
        neighbours,
        send_rows,
        noise_level,
        conv_weight,
        out_weight,
        scale_table,
        shift_table,
        cotangent[0],
    )
    return mixed[None], grad_input[None], grad_weight.reshape(K, CQ, D)


def solution(mesh):
    in_specs = (
        P(("groups", "dp"), "space", None),
        P(None, ("groups", "space")),
        P(("groups", "space"), None),
        P(("groups", "dp")),
        P(None, None, "chan"),
        P(None, "chan"),
        P(None, "chan"),
        P(None, "chan"),
        P(("groups", "dp"), "space", "chan"),
    )
    out_specs = (
        P(("groups", "dp"), "space", "chan"),
        P(("groups", "dp"), "space", "chan"),
        P("groups", "dp", "chan"),
    )
    fits = mesh.shape["space"] * mesh.shape["dp"] <= RESIDENT_SHARES
    per_device = fused_on_device if fits else on_device
    return jax.shard_map(
        per_device, mesh=mesh, in_specs=in_specs, out_specs=out_specs, check_vma=False
    )
```
